128 devices in a mesh: inner: 32 (over y, x_hi, z), outer: 4 (over x_lo, core).
Axes of the slice: x: 4 (x_hi: 2, x_lo: 2; x = x_hi * 2 + x_lo), y: 4, z: 4, core: 2. Of those that a mesh axis runs over, the one named last changes fastest.
Arguments:
- design: bfloat16 [1048576, 128], P(('inner', 'outer')), may hold values from -6 to 6
- sign_bits: int32 [1048576], P(('inner', 'outer')), may hold values from 0 to 1
- sampled: int32 [131072], P(('inner', 'outer')), may hold values from 0 to 8191
- owner_map: int32 [131072, 1], P(('inner', 'outer')), may hold values from 0 to 127; in each aligned block of 1024 rows (0 to 1023, 1024 to 2047, ...) at most 16 rows name the same one
Outputs:
- sketch_tiles: float32 [128, 128, 16, 128], P(('inner', 'outer'))
The draws below stay inside these ranges and needn't reach their ends.
Inputs may be any that keep to these rules, and one draw needn't show every extreme that they name: `owner_map`: among the 1024 samples of one block no owner appears more than 16 times, and some owner appears exactly 16 times.
All inputs are finite; a program needn't handle non-finite values.
Results may differ from the reference program's by a relative error of at most 0.0003.
Values sent between devices are 32-bit elements; how exact they have to be, the bound alone decides.
No kernel may reach another device: no remote copies, remote signals or barrier semaphores. Data moves between devices by JAX's collectives and lax.ppermute only.
A program may use at most 64 MiB of HBM per device.

```python
import math
import jax
import jax.numpy as jnp
import numpy as np
from jax import lax

COLS = 128
LANES = 128
R_DEV = 8192
M_DEV = 1024
BLOCKS = 64
ROWS = 1048576
SAMPLES = 131072
CAP = 16
N_INNER = 32
N_OUTER = 4


def plant(values, rng, low, largest):
    extent = values.shape
    place = [jax.random.randint(jax.random.fold_in(rng, axis), (), 0, extent[axis]) for axis in range(len(extent))]
    values = values.at[tuple(place)].set(low)
    longest = extent.index(max(extent))
    place[longest] = (place[longest] + 1) % extent[longest]
    return values.at[tuple(place)].set(largest)


def shard_levels(own_key, extent, shards, low, top_value):
    factor_of, own = 1.0, jax.random.fold_in(own_key, 6)
    for dim, shards_of in shards:
        heights = jnp.exp(jax.random.uniform(jax.random.fold_in(own, dim), (shards_of,), jnp.float32, low / len(shards), top_value / len(shards)))
        factor_of = factor_of * jnp.repeat(heights, extent[dim] // shards_of).reshape([-1 if axis == dim else 1 for axis in range(len(extent))])
    return factor_of


def shared_out(key, own, number, rows, number_of, top, most, slope):
    sequence = jax.random.permutation(key, number_of)
    heavy_load, usual = shares(number_of, rows * top, most, slope, True), shares(number_of, rows * top, most, slope, False)
    places = jnp.arange(number_of)

    def named(sizes, turn):
        used = int((sizes > 0).sum())
        fixed = max(1, used // 4)
        passed = fixed + (places - fixed + turn * (used - fixed)) % max(1, number_of - fixed)
        return jnp.zeros((number_of,), jnp.int32).at[sequence[jnp.where(places < fixed, places, passed)]].set(jnp.asarray(sizes, jnp.int32))

    sizes = jnp.where(number % 4 == 0, named(heavy_load, number // 4), named(usual, number - number // 4 - 1))
    mixed = jax.random.permutation(jax.random.fold_in(own, 3), number_of)
    donor, receiver = mixed[0:number_of // 2 * 2:2], mixed[1:number_of // 2 * 2:2]
    margin = jnp.minimum(sizes[donor] - 1, most - sizes[receiver]) // 2
    margin = jnp.where((donor == sequence[0]) | (receiver == sequence[0]) | (sizes[receiver] == 0), 0, jnp.maximum(margin, 0))
    passed = jax.random.randint(jax.random.fold_in(own, 4), (number_of // 2,), 0, 1 << 20) % (margin + 1)
    sizes = sizes.at[donor].add(-passed).at[receiver].add(passed)
    labels = jnp.searchsorted(jnp.cumsum(sizes), jnp.arange(rows * top), side="right").astype(jnp.int32)
    grid = labels.reshape(top, rows).T
    grid = grid[jax.random.permutation(jax.random.fold_in(own, 1), rows)]
    turn = jax.random.randint(jax.random.fold_in(own, 2), (rows, 1), 0, top)
    return jnp.take_along_axis(grid, (jnp.arange(top)[None, :] + turn) % top, axis=1)


def shares(count, total, reach, slope, full):
    loads = [(1 << 20) // math.isqrt(standing ** slope) + 1 for standing in range(1, count + 1)]
    largest = reach if full else min(reach, max(-(-total // count), total * loads[0] // sum(loads)))
    least = 1 if total - largest >= count - 1 else 0
    counts, surplus = [largest] + [least] * (count - 1), total - largest - least * (count - 1)
    while surplus > 0:
        candidates = [i for i in range(1, count) if counts[i] < largest] or [i for i in range(1, count) if counts[i] < reach]
        mass, remaining = sum([loads[i] for i in candidates]), surplus
        for i in candidates:
            addition = min(reach - counts[i], max(1, remaining * loads[i] // mass), surplus)
            counts[i] = counts[i] + addition
            surplus = surplus - addition
    return np.array(counts)


def centred(own_key, dims, scale, limit, split=(), kind=jnp.bfloat16):
    values = jax.random.normal(own_key, dims, jnp.float32) * scale
    if len(split) > 0:
        values = shard_levels(own_key, dims, split, -0.22, 0.18) * values
    return jnp.clip(values, min=-limit, max=limit).astype(kind)


def setup_inputs(seed: int = 0) -> dict:
    keys = jax.random.split(jax.random.key(seed), 5)
    design = centred(keys[0], (ROWS, COLS), 1.0, 6.0, ((0, 128),))
    sign_bits = plant(jax.random.randint(keys[1], (ROWS,), 0, 2), jax.random.fold_in(keys[1], 1), 0, 1).astype(jnp.int32)
    sampled = plant(jax.random.randint(keys[2], (SAMPLES,), 0, R_DEV), jax.random.fold_in(keys[2], 1), 0, R_DEV - 1).astype(jnp.int32)
    owner_map_keys = jax.random.split(jax.random.fold_in(keys[3], 1), SAMPLES // M_DEV)
    owner_map_turns = jax.random.permutation(jax.random.fold_in(keys[3], 3), SAMPLES // M_DEV)
    owner_map = jax.vmap(lambda own, number: shared_out(jax.random.fold_in(keys[3], 2), own, number, M_DEV, N_INNER * N_OUTER, 1, CAP, 1))(owner_map_keys, owner_map_turns).reshape((SAMPLES, 1))
    return {"design": design, "sign_bits": sign_bits, "sampled": sampled, "owner_map": owner_map}


def hadamard(order):
    left_index = jnp.arange(order, dtype=jnp.int32)[:, None]
    right_index = jnp.arange(order, dtype=jnp.int32)[None, :]
    common_bits = jnp.bitwise_and(left_index, right_index)
    parity_sum = jnp.zeros((order, order), jnp.int32)
    for bit_number in range(max(order.bit_length() - 1, 0)):
        parity_sum = parity_sum + jnp.bitwise_and(jnp.right_shift(common_bits, bit_number), 1)
    return (1 - 2 * jnp.bitwise_and(parity_sum, 1)).astype(jnp.float32)

def slot_positions(owner_block, devices):
    one_hot = (owner_block[:, :, None] == jnp.arange(devices, dtype=jnp.int32)[None, None, :]).astype(jnp.int32)
    running = jnp.cumsum(one_hot, axis=1) - 1
    return lax.optimization_barrier(jnp.sum(one_hot * running, axis=2)).astype(jnp.int32)

def reference(design, sign_bits, sampled, owner_map):
    devices = N_INNER * N_OUTER
    flipped = jnp.where(sign_bits[:, None] == 1, design, -design)
    blocked = flipped.reshape(devices, BLOCKS, LANES, COLS).astype(jnp.float32)
    highest = lax.Precision.HIGHEST
    section_one = jnp.einsum('ab,dbjc->dajc', hadamard(BLOCKS), blocked, precision=highest)
    section_two = jnp.einsum('jk,dakc->dajc', hadamard(LANES), section_one, precision=highest)
    mixed = jnp.einsum('de,eajc->dajc', hadamard(devices), section_two, precision=highest)
    mixed = mixed.reshape(devices, R_DEV, COLS)
    local_index = sampled.reshape(devices, M_DEV).astype(jnp.int32)
    picked = jax.vmap(lambda block_rows, where_from: block_rows[where_from])(mixed, local_index)
    picked = picked * (1.0 / math.sqrt(SAMPLES))
    owners = owner_map.reshape(devices, M_DEV).astype(jnp.int32)
    position = slot_positions(owners, devices)
    source = jnp.arange(devices, dtype=jnp.int32)[:, None]
    flat_slot = owners * (devices * CAP) + source * CAP + position
    result = jnp.zeros((devices * devices * CAP, COLS), jnp.float32)
    result = result.at[flat_slot.reshape(-1)].set(picked.reshape(-1, COLS))
    return result.reshape(devices, devices, CAP, COLS)
```

```python
import math

import jax
import jax.numpy as jnp
from jax import lax
from jax.experimental import pallas as pl
from jax.experimental.pallas import tpu as pltpu
from jax.sharding import PartitionSpec as P

AXES = ("inner", "outer")
DEVICES = 128
COLS = 128
LANES = 128
BLOCKS = 64
ROWS = BLOCKS * LANES
SAMPLED = 1024
CAP = 16
DATA = BLOCKS + CAP
SCALE = 1.0 / math.sqrt(SAMPLED * DEVICES)
LIMIT = 48 * 1024 * 1024


def sylvester(rows, columns):
    common = lax.broadcasted_iota(jnp.int32, (rows, columns), 0) & lax.broadcasted_iota(
        jnp.int32, (rows, columns), 1
    )
    common = common ^ (common >> 4)
    common = common ^ (common >> 2)
    common = common ^ (common >> 1)
    return (1 - 2 * (common & 1)).astype(jnp.float32)


def butterflies(values):
    half = 1
    while half < len(values):
        for start in range(0, len(values), 2 * half):
            for i in range(start, start + half):
                a, b = values[i], values[i + half]
                values[i], values[i + half] = a + b, a - b
        half *= 2
    return values


def table_kernel(sampled_ref, owner_ref, out_ref, at_slot, named):
    sampled = sampled_ref[...] + 1
    owners = owner_ref[...]
    one_hot = lax.broadcasted_iota(jnp.int32, (DEVICES, SAMPLED), 0) == owners
    one_hot16 = one_hot.astype(jnp.float32).astype(jnp.bfloat16)
    upto = (
        lax.broadcasted_iota(jnp.int32, (SAMPLED, SAMPLED), 0)
        <= lax.broadcasted_iota(jnp.int32, (SAMPLED, SAMPLED), 1)
    )
    running = jnp.dot(
        one_hot16,
        upto.astype(jnp.float32).astype(jnp.bfloat16),
        preferred_element_type=jnp.float32,
    )
    position = jnp.sum(jnp.where(one_hot, running, 0.0), axis=0, keepdims=True) - 1.0
    slots = lax.broadcasted_iota(jnp.int32, (DEVICES, SAMPLED), 0)
    at_slot[...] = jnp.where(slots == position.astype(jnp.int32), 1.0, 0.0)
    table = jnp.zeros((DEVICES, DEVICES), jnp.float32)
    for part, weight in ((sampled >> 7, 128.0), (sampled & 127, 1.0)):
        named[...] = jnp.where(one_hot, part.astype(jnp.float32), 0.0)
        table = table + weight * lax.dot_general(
            at_slot[...].astype(jnp.bfloat16),
            named[...].astype(jnp.bfloat16),
            (((1,), (1,)), ((), ())),
            preferred_element_type=jnp.float32,
        )
    out_ref[...] = table[:CAP]


def local_kernel(design_ref, signs_ref, table_ref, out_ref, mixed):
    table = table_ref[...]
    order = 2 * LANES
    matrix = sylvester(order, order)

    @pl.loop(0, BLOCKS // 2)
    def _(pair):
        signs = (2 * signs_ref[pl.ds(2 * pair, 2), :] - 1).astype(jnp.float32)
        signed = jnp.concatenate(
            [matrix[:, :LANES] * signs[0:1], matrix[:, LANES:] * signs[1:2]], axis=1
        ).astype(jnp.bfloat16)
        rows = pl.ds(pl.multiple_of(pair * order, order), order)
        mixed[rows, :] = jnp.dot(
            signed, design_ref[rows, :], preferred_element_type=jnp.float32
        )

    @pl.loop(0, order // 8)
    def _(slab):
        places = [
            pl.ds(pl.multiple_of(pair * order + slab * 8, 8), 8) for pair in range(BLOCKS // 2)
        ]
        for place, value in zip(places, butterflies([mixed[place, :] for place in places])):
            mixed[place, :] = value

    for block in range(BLOCKS):
        out_ref[pl.ds(block, COLS, stride=DATA), :] = mixed[
            block * LANES : (block + 1) * LANES, :
        ].T

    @pl.loop(0, COLS)
    def _(column):
        out_ref[pl.ds(pl.multiple_of(column * DATA + BLOCKS, 8), CAP), :] = table


def pick_kernel(column_ref, out_ref, mixed, picked):
    matrix = sylvester(DEVICES, DEVICES).astype(jnp.bfloat16)
    matrix = jnp.concatenate([matrix, matrix], axis=1)

    @pl.loop(0, BLOCKS // 2)
    def _(pair):
        high, low = [], []
        for t in range(2):
            values = column_ref[pl.ds(2 * pair + t, DEVICES, stride=DATA), :]
            top = values.astype(jnp.bfloat16)
            high.append(top)
            low.append((values - top.astype(jnp.float32)).astype(jnp.bfloat16))
        operand = jnp.concatenate(
            [jnp.concatenate(high, axis=1), jnp.concatenate(low, axis=1)], axis=0
        )
        result = jnp.dot(matrix, operand, preferred_element_type=jnp.float32)
        for t in range(2):
            rows = pl.ds(pl.multiple_of((2 * pair + t) * DEVICES, DEVICES), DEVICES)
            mixed[rows, :] = result[:, t * LANES : (t + 1) * LANES]

    @pl.loop(0, DEVICES)
    def _(source):
        table = column_ref[pl.ds(pl.multiple_of(source * DATA + BLOCKS, 8), CAP), :]
        named = table.astype(jnp.int32) - 1
        lanes = [named[t * 8 : (t + 1) * 8] & (LANES - 1) for t in range(2)]
        blocks = [named[t * 8 : (t + 1) * 8] >> 7 for t in range(2)]
        bits = [[(b >> n) & 1 == 1 for n in range(6)] for b in blocks]

        def choose(first, level):
            if level == 0:
                row = jnp.broadcast_to(
                    mixed[pl.ds(first * DEVICES + source, 1), :], (8, LANES)
                )
                return [jnp.take_along_axis(row, lane, axis=1) for lane in lanes]
            lower = choose(first, level - 1)
            upper = choose(first + (1 << (level - 1)), level - 1)
            return [
                jnp.where(bits[t][level - 1], upper[t], lower[t]) for t in range(2)
            ]

        found = choose(0, 6)
        for t in range(2):
            rows = pl.ds(pl.multiple_of(source * CAP + t * 8, 8), 8)
            picked[rows, :] = jnp.where(blocks[t] >= 0, found[t] * SCALE, 0.0)

    for group in range(CAP):
        out_ref[pl.ds(group, DEVICES, stride=CAP), :] = picked[
            group * LANES : (group + 1) * LANES, :
        ].T


def turn_kernel(arrived_ref, out_ref):
    for group in range(CAP):
        out_ref[group * LANES : (group + 1) * LANES, :] = arrived_ref[
            pl.ds(group, COLS, stride=CAP), :
        ].T


def call(kernel, rows, *args, scratch=()):
    vmem = pl.BlockSpec(memory_space=pltpu.VMEM)
    return pl.pallas_call(
        kernel,
        out_shape=jax.ShapeDtypeStruct((rows, LANES), jnp.float32),
        in_specs=[vmem] * len(args),
        out_specs=vmem,
        scratch_shapes=[pltpu.VMEM(shape, jnp.float32) for shape in scratch],
        compiler_params=pltpu.CompilerParams(vmem_limit_bytes=LIMIT),
    )(*args)


def exchange(values):
    values = values.reshape(DEVICES, -1, LANES)
    return lax.all_to_all(values, AXES, split_axis=0, concat_axis=0, tiled=True).reshape(
        -1, LANES
    )


def per_device(design, sign_bits, sampled, owner_map):
    table = call(
        table_kernel,
        CAP,
        sampled.reshape(1, SAMPLED),
        owner_map.reshape(1, SAMPLED),
        scratch=((DEVICES, SAMPLED), (DEVICES, SAMPLED)),
    )
    columns = call(
        local_kernel,
        COLS * DATA,
        design,
        sign_bits.reshape(BLOCKS, LANES),
        table,
        scratch=((ROWS, LANES),),
    )
    columns = exchange(columns)
    picked = call(pick_kernel, DEVICES * CAP, columns, scratch=((ROWS, LANES), (DEVICES * CAP, LANES)))
    picked = exchange(picked)
    tiles = call(turn_kernel, DEVICES * CAP, picked)
    return tiles.reshape(1, DEVICES, CAP, COLS)


def solution(mesh):
    in_specs = (
        P(AXES, None),
        P(AXES),
        P(AXES),
        P(AXES, None),
    )
    out_specs = P(AXES, None, None, None)
    return jax.shard_map(
        per_device, mesh=mesh, in_specs=in_specs, out_specs=out_specs, check_vma=False
    )
```

```python
import math

import jax
import jax.numpy as jnp
from jax import lax
from jax.experimental import pallas as pl
from jax.experimental.pallas import tpu as pltpu
from jax.sharding import PartitionSpec as P

AXES = ("inner", "outer")
DEVICES = 128
COLS = 128
LANES = 128
BLOCKS = 64
ROWS = BLOCKS * LANES
SAMPLED = 1024
CAP = 16
LISTED = SAMPLED // LANES
TABLE = LISTED + CAP
SCALE = 1.0 / math.sqrt(SAMPLED * DEVICES)
PARTS = 8
F32 = jnp.float32
BF16 = jnp.bfloat16


def iota(shape, axis):
    return lax.broadcasted_iota(jnp.int32, shape, axis)


def sylvester(rows, columns):
    common = iota((rows, columns), 0) & iota((rows, columns), 1)
    common = common ^ (common >> 4)
    common = common ^ (common >> 2)
    common = common ^ (common >> 1)
    return (1 - 2 * (common & 1)).astype(F32)


def butterflies(values):
    half = 1
    while half < len(values):
        for start in range(0, len(values), 2 * half):
            for i in range(start, start + half):
                a, b = values[i], values[i + half]
                values[i], values[i + half] = a + b, a - b
        half *= 2
    return values


def transform_in_place(ref, places):
    for place, value in zip(places, butterflies([ref[place, :] for place in places])):
        ref[place, :] = value


def aligned(start, size):
    return pl.ds(pl.multiple_of(start, 8), size)


def table_kernel(sampled_ref, owner_ref, out_ref, at_slot, named):
    owners = owner_ref[...]
    one_hot = iota((DEVICES, SAMPLED), 0) == owners
    upto = iota((SAMPLED, SAMPLED), 0) <= iota((SAMPLED, SAMPLED), 1)
    running = jnp.dot(
        one_hot.astype(F32).astype(BF16), upto.astype(F32).astype(BF16), preferred_element_type=F32
    )
    position = jnp.sum(jnp.where(one_hot, running, 0.0), axis=0, keepdims=True) - 1.0
    at_slot[...] = jnp.where(
        iota((DEVICES, SAMPLED), 0) == position.astype(jnp.int32), 1.0, 0.0
    )
    place = iota((1, SAMPLED), 1) + 1
    table = jnp.zeros((DEVICES, DEVICES), F32)
    for part, weight in ((place >> 7, 128.0), (place & 127, 1.0)):
        named[...] = jnp.where(one_hot, part.astype(F32), 0.0)
        table = table + weight * lax.dot_general(
            at_slot[...].astype(BF16),
            named[...].astype(BF16),
            (((1,), (1,)), ((), ())),
            preferred_element_type=F32,
        )
    for row in range(LISTED):
        out_ref[row : row + 1, :] = sampled_ref[:, row * LANES : (row + 1) * LANES].astype(F32)
    out_ref[LISTED:, :] = table[:CAP]


def local_kernel(design_hbm, signs_hbm, out_ref, design, signs, mixed, turned, sems, sign_sem):
    chunk = ROWS // PARTS
    copies = [
        pltpu.make_async_copy(
            design_hbm.at[pl.ds(n * chunk, chunk)], design.at[pl.ds(n * chunk, chunk)], sems.at[n]
        )
        for n in range(PARTS)
    ]
    sign_copy = pltpu.make_async_copy(signs_hbm, signs, sign_sem)
    sign_copy.start()
    for copy in copies:
        copy.start()
    order = 2 * LANES
    pairs = BLOCKS // 2
    matrix = sylvester(order, order)
    sign_copy.wait()
    for n in range(PARTS):
        copies[n].wait()
        for pair in range(n * pairs // PARTS, (n + 1) * pairs // PARTS):
            sign = (2 * signs[2 * pair : 2 * pair + 2, :] - 1).astype(F32)
            signed = jnp.concatenate(
                [matrix[:, :LANES] * sign[0:1], matrix[:, LANES:] * sign[1:2]], axis=1
            ).astype(BF16)
            rows = pl.ds(pair * order, order)
            mixed[rows, :] = jnp.dot(signed, design[rows, :], preferred_element_type=F32)

    @pl.loop(0, order // 8)
    def _(slab):
        transform_in_place(
            mixed, [aligned(pair * order + slab * 8, 8) for pair in range(pairs)]
        )

    for block in range(BLOCKS):
        rows = slice(block * LANES, (block + 1) * LANES)
        turned[rows, :] = mixed[rows, :].T

    @pl.loop(0, COLS, unroll=4)
    def _(column):
        for part in range(BLOCKS // 8):
            out_ref[aligned(column * BLOCKS + part * 8, 8), :] = turned[
                pl.ds(part * 8 * COLS + column, 8, stride=COLS), :
            ]


def gather_rows(parts):
    row = iota((8, LANES), 0)
    step = 1
    while len(parts) > 1:
        upper = (row & step) != 0
        parts = [
            jnp.where(upper, b, a) + pltpu.roll(jnp.where(upper, a, b), step, 0)
            for a, b in zip(parts[0::2], parts[1::2])
        ]
        step *= 2
    return parts[0]


def pick_kernel(column_hbm, table_ref, out_ref, mixed, found, picked, sems):
    copies = [
        pltpu.make_async_copy(
            column_hbm.at[:, pl.ds(8 * n, 8), :], mixed.at[:, pl.ds(8 * n, 8), :], sems.at[n]
        )
        for n in range(PARTS)
    ]
    for copy in copies:
        copy.start()
    for n in range(PARTS):
        copies[n].wait()
        rows = pl.ds(8 * n, 8)

        @pl.loop(0, 8)
        def _(low):
            places = [high * 8 + low for high in range(16)]
            values = butterflies([mixed[place, rows, :] for place in places])
            for place, value in zip(places, values):
                mixed[place, rows, :] = value

        @pl.loop(0, 16)
        def _(high):
            places = [high * 8 + low for low in range(8)]
            values = butterflies([mixed[place, rows, :] for place in places])
            for place, value in zip(places, values):
                mixed[place, rows, :] = value

    half = BLOCKS // 2
    place = iota((2 * LANES, LANES), 0).astype(F32).astype(BF16)
    row8 = iota((8, LANES), 0)
    one, zero = jnp.ones((), BF16), jnp.zeros((), BF16)

    @pl.loop(0, DEVICES, unroll=2)
    def _(source):
        listed = table_ref[aligned(source * TABLE, LISTED), :].astype(jnp.int32)
        key = ((listed & (LANES - 1)) + ((listed >> 12) << 7)).astype(F32)
        block = (listed >> 7) & (half - 1)
        values = mixed[source]
        top = values.astype(BF16)
        rest = (values - top.astype(F32)).astype(BF16)
        operand = jnp.concatenate(
            [
                jnp.concatenate([top[:half], top[half:]], axis=1),
                jnp.concatenate([rest[:half], rest[half:]], axis=1),
            ],
            axis=0,
        )
        one_hot = jnp.concatenate(
            [
                jnp.where(
                    place == jnp.broadcast_to(key[r : r + 1], (2 * LANES, LANES)).astype(BF16),
                    one,
                    zero,
                )
                for r in range(LISTED)
            ],
            axis=1,
        )
        result = jnp.dot(operand, one_hot, preferred_element_type=F32)
        result = result[:half] + result[half:]
        parts = []
        for r in range(LISTED):
            wanted = jnp.broadcast_to(block[r : r + 1], (8, LANES))
            part = jnp.zeros((8, LANES), F32)
            for g in range(half // 8):
                part = jnp.where(
                    wanted == row8 + 8 * g,
                    result[8 * g : 8 * g + 8, r * LANES : (r + 1) * LANES],
                    part,
                )
            parts.append(part)
        found = gather_rows(parts)

        slots = table_ref[aligned(source * TABLE + LISTED, CAP), :].astype(jnp.int32) - 1
        for t in range(2):
            slot = slots[8 * t : 8 * t + 8]
            lane = slot & (LANES - 1)
            rows = [
                jnp.take_along_axis(jnp.broadcast_to(found[r : r + 1], (8, LANES)), lane, axis=1)
                for r in range(LISTED)
            ]
            for n in range(3):
                odd = (slot >> (7 + n)) & 1 == 1
                rows = [jnp.where(odd, b, a) for a, b in zip(rows[0::2], rows[1::2])]
            picked[aligned(source * CAP + 8 * t, 8), :] = jnp.where(
                slot >= 0, rows[0] * SCALE, 0.0
            )

    for group in range(CAP):
        out_ref[pl.ds(group, DEVICES, stride=CAP), :] = picked[
            group * LANES : (group + 1) * LANES, :
        ].T


def turn_kernel(arrived_ref, out_ref):
    for group in range(CAP):
        out_ref[group * LANES : (group + 1) * LANES, :] = arrived_ref[
            pl.ds(group, COLS, stride=CAP), :
        ].T


HBM = pl.BlockSpec(memory_space=pl.ANY)
VMEM = pl.BlockSpec(memory_space=pltpu.VMEM)


def call(kernel, rows, specs, *args, scratch=(), limit=24):
    return pl.pallas_call(
        kernel,
        out_shape=jax.ShapeDtypeStruct((rows, LANES), F32),
        in_specs=specs,
        out_specs=VMEM,
        scratch_shapes=scratch,
        compiler_params=pltpu.CompilerParams(vmem_limit_bytes=limit * 1024 * 1024),
    )(*args)


def exchange(values):
    values = values.reshape(DEVICES, -1, LANES)
    return lax.all_to_all(values, AXES, split_axis=0, concat_axis=0, tiled=True)


def gather_tables(table):
    inner = lax.axis_size("inner")
    near = [[g * 4 + i for i in range(4)] for g in range(inner // 4)]
    far = [[g + 4 * i for i in range(inner // 4)] for g in range(4)]
    table = lax.all_gather(table, "outer", axis=0, tiled=True)
    table = lax.all_gather(table, "inner", axis=0, tiled=True, axis_index_groups=near)
    return lax.all_gather(table, "inner", axis=0, tiled=True, axis_index_groups=far)


def per_device(design, sign_bits, sampled, owner_map):
    vmem, dma = pltpu.VMEM, pltpu.SemaphoreType.DMA
    table = call(
        table_kernel,
        TABLE,
        [VMEM, VMEM],
        sampled.reshape(1, SAMPLED),
        owner_map.reshape(1, SAMPLED),
        scratch=[vmem((DEVICES, SAMPLED), F32), vmem((DEVICES, SAMPLED), F32)],
    )
    tables = gather_tables(table)
    columns = call(
        local_kernel,
        COLS * BLOCKS,
        [HBM, HBM],
        design,
        sign_bits.reshape(BLOCKS, LANES),
        scratch=[
            vmem((ROWS, LANES), BF16),
            vmem((BLOCKS, LANES), jnp.int32),
            vmem((ROWS, LANES), F32),
            vmem((ROWS, LANES), F32),
            dma((PARTS,)),
            dma(()),
        ],
    )
    picked = call(
        pick_kernel,
        DEVICES * CAP,
        [HBM, VMEM],
        exchange(columns),
        tables,
        scratch=[
            vmem((DEVICES, BLOCKS, LANES), F32),
            vmem((8, LANES), F32),
            vmem((DEVICES * CAP, LANES), F32),
            dma((PARTS,)),
        ],
    )
    tiles = call(turn_kernel, DEVICES * CAP, [VMEM], exchange(picked).reshape(-1, LANES))
    return tiles.reshape(1, DEVICES, CAP, COLS)


def solution(mesh):
    in_specs = (
        P(AXES, None),
        P(AXES),
        P(AXES),
        P(AXES, None),
    )
    out_specs = P(AXES, None, None, None)
    return jax.shard_map(
        per_device, mesh=mesh, in_specs=in_specs, out_specs=out_specs, check_vma=False
    )
```

```python
import math

import jax
import jax.numpy as jnp
from jax import lax
from jax.experimental import pallas as pl
from jax.experimental.pallas import tpu as pltpu
from jax.sharding import PartitionSpec as P

AXES = ("inner", "outer")
DEVICES = 128
COLS = 128
LANES = 128
BLOCKS = 64
ROWS = BLOCKS * LANES
SAMPLED = 1024
CAP = 16
LISTED = SAMPLED // LANES
TABLE = LISTED + CAP
SCALE = 1.0 / math.sqrt(SAMPLED * DEVICES)
PARTS = 8
GROUP = 8
F32 = jnp.float32
BF16 = jnp.bfloat16


def iota(shape, axis):
    return lax.broadcasted_iota(jnp.int32, shape, axis)


def sylvester(rows, columns):
    common = iota((rows, columns), 0) & iota((rows, columns), 1)
    common = common ^ (common >> 4)
    common = common ^ (common >> 2)
    common = common ^ (common >> 1)
    return (1 - 2 * (common & 1)).astype(F32)


def butterflies(values):
    half = 1
    while half < len(values):
        for start in range(0, len(values), 2 * half):
            for i in range(start, start + half):
                a, b = values[i], values[i + half]
                values[i], values[i + half] = a + b, a - b
        half *= 2
    return values


def transform_in_place(ref, places):
    for place, value in zip(places, butterflies([ref[place, :] for place in places])):
        ref[place, :] = value


def aligned(start, size):
    return pl.ds(pl.multiple_of(start, 8), size)


def slot_table(sampled, owners, at_slot, named):
    one_hot = iota((DEVICES, SAMPLED), 0) == owners
    upto = iota((SAMPLED, SAMPLED), 0) <= iota((SAMPLED, SAMPLED), 1)
    running = jnp.dot(
        one_hot.astype(F32).astype(BF16), upto.astype(F32).astype(BF16), preferred_element_type=F32
    )
    position = jnp.sum(jnp.where(one_hot, running, 0.0), axis=0, keepdims=True) - 1.0
    at_slot[...] = jnp.where(
        iota((DEVICES, SAMPLED), 0) == position.astype(jnp.int32), 1.0, 0.0
    )
    place = iota((1, SAMPLED), 1) + 1
    table = jnp.zeros((DEVICES, DEVICES), F32)
    for part, weight in ((place >> 7, 128.0), (place & 127, 1.0)):
        named[...] = jnp.where(one_hot, part.astype(F32), 0.0)
        table = table + weight * lax.dot_general(
            at_slot[...].astype(BF16),
            named[...].astype(BF16),
            (((1,), (1,)), ((), ())),
            preferred_element_type=F32,
        )
    listed = [sampled[:, row * LANES : (row + 1) * LANES].astype(F32) for row in range(LISTED)]
    return jnp.concatenate(listed + [table[:CAP]], axis=0)


def local_kernel(
    design_hbm, signs_hbm, sampled_hbm, owner_hbm, out_ref, table_ref,
    design, signs, sampled, owners, at_slot, named, mixed, turned, sems, small_sems,
):
    chunk = ROWS // PARTS
    small = [
        pltpu.make_async_copy(source, target, small_sems.at[n])
        for n, (source, target) in enumerate(
            ((sampled_hbm, sampled), (owner_hbm, owners), (signs_hbm, signs))
        )
    ]
    copies = [
        pltpu.make_async_copy(
            design_hbm.at[pl.ds(n * chunk, chunk)], design.at[pl.ds(n * chunk, chunk)], sems.at[n]
        )
        for n in range(PARTS)
    ]
    for copy in small + copies:
        copy.start()
    order = 2 * LANES
    pairs = BLOCKS // 2
    matrix = sylvester(order, order)
    for copy in small:
        copy.wait()
    table_ref[...] = slot_table(sampled[...], owners[...], at_slot, named)
    for n in range(PARTS):
        copies[n].wait()
        for pair in range(n * pairs // PARTS, (n + 1) * pairs // PARTS):
            sign = (2 * signs[2 * pair : 2 * pair + 2, :] - 1).astype(F32)
            signed = jnp.concatenate(
                [matrix[:, :LANES] * sign[0:1], matrix[:, LANES:] * sign[1:2]], axis=1
            ).astype(BF16)
            rows = pl.ds(pair * order, order)
            mixed[rows, :] = jnp.dot(signed, design[rows, :], preferred_element_type=F32)

    @pl.loop(0, order // 8)
    def _(slab):
        transform_in_place(
            mixed, [aligned(pair * order + slab * 8, 8) for pair in range(pairs)]
        )

    for block in range(BLOCKS):
        rows = slice(block * LANES, (block + 1) * LANES)
        turned[rows, :] = mixed[rows, :].T

    @pl.loop(0, COLS, unroll=4)
    def _(column):
        for part in range(BLOCKS // 8):
            out_ref[aligned(column * BLOCKS + part * 8, 8), :] = turned[
                pl.ds(part * 8 * COLS + column, 8, stride=COLS), :
            ]


def gather_rows(parts):
    row = iota((8, LANES), 0)
    step = 1
    while len(parts) > 1:
        upper = (row & step) != 0
        parts = [
            jnp.where(upper, b, a) + pltpu.roll(jnp.where(upper, a, b), step, 0)
            for a, b in zip(parts[0::2], parts[1::2])
        ]
        step *= 2
    return parts[0]


def pick_kernel(me_ref, column_hbm, table_ref, out_ref, mixed, found, picked, sems):
    me = me_ref[0]
    copies = [
        pltpu.make_async_copy(
            column_hbm.at[:, pl.ds(8 * n, 8), :], mixed.at[:, pl.ds(8 * n, 8), :], sems.at[n]
        )
        for n in range(PARTS)
    ]
    for copy in copies:
        copy.start()
    for n in range(PARTS):
        copies[n].wait()
        rows = pl.ds(8 * n, 8)

        @pl.loop(0, 8)
        def _(low):
            places = [high * 8 + low for high in range(16)]
            values = butterflies([mixed[place, rows, :] for place in places])
            for place, value in zip(places, values):
                mixed[place, rows, :] = value

        @pl.loop(0, 16)
        def _(high):
            places = [high * 8 + low for low in range(8)]
            values = butterflies([mixed[place, rows, :] for place in places])
            for place, value in zip(places, values):
                mixed[place, rows, :] = value

    place = iota((LANES, LANES), 0).astype(F32).astype(BF16)
    row8 = iota((8, LANES), 0)
    one, zero = jnp.ones((), BF16), jnp.zeros((), BF16)

    def pick(source):
        listed = table_ref[aligned((source ^ me) * TABLE, LISTED), :].astype(jnp.int32)
        key = (listed & (LANES - 1)).astype(F32)
        block = listed >> 7
        values = mixed[source]
        top = values.astype(BF16)
        operand = jnp.concatenate([top, (values - top.astype(F32)).astype(BF16)], axis=0)
        parts = []
        for r in range(LISTED):
            mine = jnp.broadcast_to(key[r : r + 1], (16, LANES)).astype(BF16)
            one_hot = jnp.concatenate(
                [jnp.where(place[16 * g : 16 * g + 16] == mine, one, zero) for g in range(8)],
                axis=0,
            )
            result = jnp.dot(operand, one_hot, preferred_element_type=F32)
            wanted = jnp.broadcast_to(block[r : r + 1], (8, LANES))
            values = [
                result[8 * g : 8 * g + 8] + result[BLOCKS + 8 * g : BLOCKS + 8 * g + 8]
                for g in range(8)
            ]
            for n in range(3, 6):
                odd = (wanted >> n) & 1 == 1
                values = [jnp.where(odd, b, a) for a, b in zip(values[0::2], values[1::2])]
            parts.append(jnp.where(wanted & 7 == row8, values[0], 0.0))
        found[aligned(source * LISTED, LISTED), :] = gather_rows(parts)

    def place_in_slots(source):
        slots = table_ref[aligned((source ^ me) * TABLE + LISTED, CAP), :].astype(jnp.int32) - 1
        here = found[aligned(source * LISTED, LISTED), :]
        for t in range(2):
            slot = slots[8 * t : 8 * t + 8]
            lane = slot & (LANES - 1)
            rows = [
                jnp.take_along_axis(jnp.broadcast_to(here[r : r + 1], (8, LANES)), lane, axis=1)
                for r in range(LISTED)
            ]
            for n in range(3):
                odd = (slot >> (7 + n)) & 1 == 1
                rows = [jnp.where(odd, b, a) for a, b in zip(rows[0::2], rows[1::2])]
            picked[aligned(source * CAP + 8 * t, 8), :] = jnp.where(
                slot >= 0, rows[0] * SCALE, 0.0
            )

    for n in range(GROUP):
        pick(n)

    @pl.loop(1, DEVICES // GROUP)
    def _(group):
        for n in range(GROUP):
            place_in_slots((group - 1) * GROUP + n)
            pick(group * GROUP + n)

    for n in range(GROUP):
        place_in_slots(DEVICES - GROUP + n)

    for group in range(CAP):
        out_ref[pl.ds(group, DEVICES, stride=CAP), :] = picked[
            group * LANES : (group + 1) * LANES, :
        ].T


def turn_kernel(arrived_ref, out_ref):
    for group in range(CAP):
        out_ref[group * LANES : (group + 1) * LANES, :] = arrived_ref[
            pl.ds(group, COLS, stride=CAP), :
        ].T


HBM = pl.BlockSpec(memory_space=pl.ANY)
VMEM = pl.BlockSpec(memory_space=pltpu.VMEM)
SMEM = pl.BlockSpec(memory_space=pltpu.SMEM)


def call(kernel, rows, specs, *args, scratch=(), limit=24):
    shapes = [jax.ShapeDtypeStruct((n, LANES), F32) for n in rows]
    return pl.pallas_call(
        kernel,
        out_shape=shapes,
        in_specs=specs,
        out_specs=[VMEM] * len(rows),
        scratch_shapes=scratch,
        compiler_params=pltpu.CompilerParams(vmem_limit_bytes=limit * 1024 * 1024),
    )(*args)


def local_call(design, sign_bits, sampled, owner_map):
    vmem, dma = pltpu.VMEM, pltpu.SemaphoreType.DMA
    return call(
        local_kernel,
        [COLS * BLOCKS, TABLE],
        [HBM] * 4,
        design,
        sign_bits.reshape(BLOCKS, LANES),
        sampled.reshape(1, SAMPLED),
        owner_map.reshape(1, SAMPLED),
        scratch=[
            vmem((ROWS, LANES), BF16),
            vmem((BLOCKS, LANES), jnp.int32),
            vmem((1, SAMPLED), jnp.int32),
            vmem((1, SAMPLED), jnp.int32),
            vmem((DEVICES, SAMPLED), F32),
            vmem((DEVICES, SAMPLED), F32),
            vmem((ROWS, LANES), F32),
            vmem((ROWS, LANES), F32),
            dma((PARTS,)),
            dma((3,)),
        ],
    )


def pick_call(me, columns, tables):
    vmem, dma = pltpu.VMEM, pltpu.SemaphoreType.DMA
    return call(
        pick_kernel,
        [DEVICES * CAP],
        [SMEM, HBM, VMEM],
        me,
        columns,
        tables,
        scratch=[
            vmem((DEVICES, BLOCKS, LANES), F32),
            vmem((DEVICES * LISTED, LANES), F32),
            vmem((DEVICES * CAP, LANES), F32),
            dma((PARTS,)),
        ],
    )[0]


def exchange(values):
    values = values.reshape(DEVICES, -1, LANES)
    return lax.all_to_all(values, AXES, split_axis=0, concat_axis=0, tiled=True)


def gather_tables(table):
    steps = (("outer", range(1, 4)), ("inner", range(1, 4)), ("inner", range(4, 32, 4)))
    for axis, others in steps:
        size = lax.axis_size(axis)
        pieces = [
            lax.ppermute(table, axis, [(place, place ^ other) for place in range(size)])
            for other in others
        ]
        table = jnp.concatenate([table] + pieces, axis=0)
    return table


def per_device(design, sign_bits, sampled, owner_map):
    me = lax.axis_index("inner") * lax.axis_size("outer") + lax.axis_index("outer")
    columns, table = local_call(design, sign_bits, sampled, owner_map)
    tables = gather_tables(table)
    picked = pick_call(me.astype(jnp.int32).reshape(1), exchange(columns), tables)
    (tiles,) = call(turn_kernel, [DEVICES * CAP], [VMEM], exchange(picked).reshape(-1, LANES))
    return tiles.reshape(1, DEVICES, CAP, COLS)


def solution(mesh):
    in_specs = (
        P(AXES, None),
        P(AXES),
        P(AXES),
        P(AXES, None),
    )
    out_specs = P(AXES, None, None, None)
    return jax.shard_map(
        per_device, mesh=mesh, in_specs=in_specs, out_specs=out_specs, check_vma=False
    )
```

```python
import math

import jax
import jax.numpy as jnp
from jax import lax
from jax.experimental import pallas as pl
from jax.experimental.pallas import tpu as pltpu
from jax.sharding import PartitionSpec as P

AXES = ("inner", "outer")
DEVICES = 128
COLS = 128
LANES = 128
BLOCKS = 64
ROWS = BLOCKS * LANES
SAMPLED = 1024
CAP = 16
LISTED = SAMPLED // LANES
TABLE = 16
DATA = BLOCKS + TABLE
SCALE = 1.0 / math.sqrt(SAMPLED * DEVICES)
PARTS = 8
GROUP = 8
F32 = jnp.float32
BF16 = jnp.bfloat16


def iota(shape, axis):
    return lax.broadcasted_iota(jnp.int32, shape, axis)


def sylvester(rows, columns):
    common = iota((rows, columns), 0) & iota((rows, columns), 1)
    common = common ^ (common >> 4)
    common = common ^ (common >> 2)
    common = common ^ (common >> 1)
    return (1 - 2 * (common & 1)).astype(F32)


def butterflies(values):
    half = 1
    while half < len(values):
        for start in range(0, len(values), 2 * half):
            for i in range(start, start + half):
                a, b = values[i], values[i + half]
                values[i], values[i + half] = a + b, a - b
        half *= 2
    return values


def transform_in_place(ref, places):
    for place, value in zip(places, butterflies([ref[place, :] for place in places])):
        ref[place, :] = value


def aligned(start, size):
    return pl.ds(pl.multiple_of(start, 8), size)


def slot_table(sampled, owners, at_row, named):
    one_hot = iota((DEVICES, SAMPLED), 0) == owners
    one_hot16 = one_hot.astype(F32).astype(BF16)
    upto = iota((SAMPLED, SAMPLED), 0) <= iota((SAMPLED, SAMPLED), 1)
    running = jnp.dot(one_hot16, upto.astype(F32).astype(BF16), preferred_element_type=F32)
    counts = jnp.broadcast_to(running[:, SAMPLED - 1 :], (DEVICES, LANES))
    below = iota((DEVICES, DEVICES), 1) < iota((DEVICES, DEVICES), 0)
    starts = jnp.dot(
        below.astype(F32).astype(BF16), counts.astype(BF16), preferred_element_type=F32
    )
    place = jnp.sum(
        jnp.where(one_hot, running + starts[:, :1], 0.0), axis=0, keepdims=True
    ).astype(jnp.int32) - 1
    at_row[...] = jnp.where(iota((DEVICES, SAMPLED), 0) == place >> 7, 1.0, 0.0)
    at_lane = iota((DEVICES, SAMPLED), 0) == place & (LANES - 1)
    table = jnp.zeros((DEVICES, LANES), F32)
    for part, weight in ((sampled >> 7, 128.0), (sampled & 127, 1.0)):
        named[...] = jnp.where(at_lane, part.astype(F32), 0.0)
        table = table + weight * lax.dot_general(
            at_row[...].astype(BF16),
            named[...].astype(BF16),
            (((1,), (1,)), ((), ())),
            preferred_element_type=F32,
        )
    return jnp.concatenate(
        [
            table[:LISTED],
            starts.T[:1],
            counts.T[:1],
            jnp.zeros((TABLE - LISTED - 2, LANES), F32),
        ],
        axis=0,
    )


def local_kernel(
    design_hbm, signs_hbm, sampled_hbm, owner_hbm, out_ref,
    design, signs, sampled, owners, at_row, named, mixed, turned, sems, small_sems,
):
    chunk = ROWS // PARTS
    small = [
        pltpu.make_async_copy(source, target, small_sems.at[n])
        for n, (source, target) in enumerate(
            ((sampled_hbm, sampled), (owner_hbm, owners), (signs_hbm, signs))
        )
    ]
    copies = [
        pltpu.make_async_copy(
            design_hbm.at[pl.ds(n * chunk, chunk)], design.at[pl.ds(n * chunk, chunk)], sems.at[n]
        )
        for n in range(PARTS)
    ]
    for copy in small + copies:
        copy.start()
    order = 2 * LANES
    pairs = BLOCKS // 2
    matrix = sylvester(order, order)
    for copy in small:
        copy.wait()
    table = slot_table(sampled[...], owners[...], at_row, named)
    for n in range(PARTS):
        copies[n].wait()
        for pair in range(n * pairs // PARTS, (n + 1) * pairs // PARTS):
            sign = (2 * signs[2 * pair : 2 * pair + 2, :] - 1).astype(F32)
            signed = jnp.concatenate(
                [matrix[:, :LANES] * sign[0:1], matrix[:, LANES:] * sign[1:2]], axis=1
            ).astype(BF16)
            rows = pl.ds(pair * order, order)
            mixed[rows, :] = jnp.dot(signed, design[rows, :], preferred_element_type=F32)

    @pl.loop(0, order // 8)
    def _(slab):
        transform_in_place(
            mixed, [aligned(pair * order + slab * 8, 8) for pair in range(pairs)]
        )

    for block in range(BLOCKS):
        rows = slice(block * LANES, (block + 1) * LANES)
        turned[rows, :] = mixed[rows, :].T

    @pl.loop(0, COLS, unroll=4)
    def _(column):
        for part in range(BLOCKS // 8):
            out_ref[aligned(column * DATA + part * 8, 8), :] = turned[
                pl.ds(part * 8 * COLS + column, 8, stride=COLS), :
            ]
        out_ref[aligned(column * DATA + BLOCKS, TABLE), :] = table


def gather_rows(parts):
    row = iota((8, LANES), 0)
    step = 1
    while len(parts) > 1:
        upper = (row & step) != 0
        parts = [
            jnp.where(upper, b, a) + pltpu.roll(jnp.where(upper, a, b), step, 0)
            for a, b in zip(parts[0::2], parts[1::2])
        ]
        step *= 2
    return parts[0]


def pick_kernel(column_ref, out_ref, mixed, found, picked):
    @pl.loop(0, BLOCKS)
    def _(step):
        part, low = step // 8, step % 8
        places = [
            aligned((high * 8 + low) * DATA + part * 8, 8) for high in range(16)
        ]
        values = butterflies([column_ref[place, :] for place in places])
        for high, value in enumerate(values):
            mixed[high * 8 + low, aligned(part * 8, 8), :] = value

    @pl.loop(0, 2 * BLOCKS)
    def _(step):
        part, high = step // 16, step % 16
        rows = aligned(part * 8, 8)
        values = butterflies([mixed[high * 8 + low, rows, :] for low in range(8)])
        for low, value in enumerate(values):
            mixed[high * 8 + low, rows, :] = value

    place = iota((LANES, LANES), 0).astype(F32).astype(BF16)
    row8 = iota((8, LANES), 0)
    one, zero = jnp.ones((), BF16), jnp.zeros((), BF16)

    def pick(source):
        listed = column_ref[aligned(source * DATA + BLOCKS, LISTED), :].astype(jnp.int32)
        key = (listed & (LANES - 1)).astype(F32)
        block = listed >> 7
        values = mixed[source]
        top = values.astype(BF16)
        operand = jnp.concatenate([top, (values - top.astype(F32)).astype(BF16)], axis=0)
        parts = []
        for r in range(LISTED):
            mine = jnp.broadcast_to(key[r : r + 1], (16, LANES)).astype(BF16)
            one_hot = jnp.concatenate(
                [jnp.where(place[16 * g : 16 * g + 16] == mine, one, zero) for g in range(8)],
                axis=0,
            )
            result = jnp.dot(operand, one_hot, preferred_element_type=F32)
            wanted = jnp.broadcast_to(block[r : r + 1], (8, LANES))
            values = [
                result[8 * g : 8 * g + 8] + result[BLOCKS + 8 * g : BLOCKS + 8 * g + 8]
                for g in range(8)
            ]
            for n in range(3, 6):
                odd = (wanted >> n) & 1 == 1
                values = [jnp.where(odd, b, a) for a, b in zip(values[0::2], values[1::2])]
            parts.append(jnp.where(wanted & 7 == row8, values[0], 0.0))
        found[aligned(source * LISTED, LISTED), :] = gather_rows(parts)

    def place_in_slots(source):
        spans = column_ref[aligned(source * DATA + BLOCKS + LISTED, 8), :].astype(jnp.int32)
        start, count = (jnp.broadcast_to(spans[n : n + 1], (8, LANES)) for n in range(2))
        here = found[aligned(source * LISTED, LISTED), :]
        for t in range(2):
            position = row8 + 8 * t
            slot = start + position
            lane = slot & (LANES - 1)
            rows = [
                jnp.take_along_axis(jnp.broadcast_to(here[r : r + 1], (8, LANES)), lane, axis=1)
                for r in range(LISTED)
            ]
            for n in range(3):
                odd = (slot >> (7 + n)) & 1 == 1
                rows = [jnp.where(odd, b, a) for a, b in zip(rows[0::2], rows[1::2])]
            picked[aligned(source * CAP + 8 * t, 8), :] = jnp.where(
                position < count, rows[0] * SCALE, 0.0
            )

    for n in range(GROUP):
        pick(n)

    @pl.loop(1, DEVICES // GROUP)
    def _(group):
        for n in range(GROUP):
            place_in_slots((group - 1) * GROUP + n)
            pick(group * GROUP + n)

    for n in range(GROUP):
        place_in_slots(DEVICES - GROUP + n)

    for group in range(CAP):
        out_ref[pl.ds(group, DEVICES, stride=CAP), :] = picked[
            group * LANES : (group + 1) * LANES, :
        ].T


def turn_kernel(arrived_ref, out_ref):
    for group in range(CAP):
        out_ref[group * LANES : (group + 1) * LANES, :] = arrived_ref[
            pl.ds(group, COLS, stride=CAP), :
        ].T


HBM = pl.BlockSpec(memory_space=pltpu.HBM)
VMEM = pl.BlockSpec(memory_space=pltpu.VMEM)


def call(kernel, rows, specs, *args, scratch=(), limit=24):
    shapes = [jax.ShapeDtypeStruct((n, LANES), F32) for n in rows]
    return pl.pallas_call(
        kernel,
        out_shape=shapes,
        in_specs=specs,
        out_specs=[VMEM] * len(rows),
        scratch_shapes=scratch,
        compiler_params=pltpu.CompilerParams(vmem_limit_bytes=limit * 1024 * 1024),
    )(*args)


def local_call(design, sign_bits, sampled, owner_map):
    vmem, dma = pltpu.VMEM, pltpu.SemaphoreType.DMA
    return call(
        local_kernel,
        [COLS * DATA],
        [HBM] * 4,
        design,
        sign_bits.reshape(BLOCKS, LANES),
        sampled.reshape(1, SAMPLED),
        owner_map.reshape(1, SAMPLED),
        scratch=[
            vmem((ROWS, LANES), BF16),
            vmem((BLOCKS, LANES), jnp.int32),
            vmem((1, SAMPLED), jnp.int32),
            vmem((1, SAMPLED), jnp.int32),
            vmem((DEVICES, SAMPLED), F32),
            vmem((DEVICES, SAMPLED), F32),
            vmem((ROWS, LANES), F32),
            vmem((ROWS, LANES), F32),
            dma((PARTS,)),
            dma((3,)),
        ],
    )[0]


def pick_call(columns):
    return call(
        pick_kernel,
        [DEVICES * CAP],
        [VMEM],
        columns,
        scratch=[
            pltpu.VMEM((DEVICES, BLOCKS, LANES), F32),
            pltpu.VMEM((DEVICES * LISTED, LANES), F32),
            pltpu.VMEM((DEVICES * CAP, LANES), F32),
        ],
    )[0]


def exchange(values):
    values = values.reshape(DEVICES, -1, LANES)
    return lax.all_to_all(values, AXES, split_axis=0, concat_axis=0, tiled=True).reshape(
        -1, LANES
    )


def per_device(design, sign_bits, sampled, owner_map):
    columns = exchange(local_call(design, sign_bits, sampled, owner_map))
    picked = exchange(pick_call(columns))
    (tiles,) = call(turn_kernel, [DEVICES * CAP], [VMEM], picked)
    return tiles.reshape(1, DEVICES, CAP, COLS)


def solution(mesh):
    in_specs = (
        P(AXES, None),
        P(AXES),
        P(AXES),
        P(AXES, None),
    )
    out_specs = P(AXES, None, None, None)
    return jax.shard_map(
        per_device, mesh=mesh, in_specs=in_specs, out_specs=out_specs, check_vma=False
    )
```

```python
import math

import jax
import jax.numpy as jnp
from jax import lax
from jax.experimental import pallas as pl
from jax.experimental.pallas import tpu as pltpu
from jax.sharding import PartitionSpec as P

AXES = ("inner", "outer")
DEVICES = 128
COLS = 128
LANES = 128
BLOCKS = 64
ROWS = BLOCKS * LANES
SAMPLED = 1024
CAP = 16
LISTED = SAMPLED // LANES
TABLE = 8
DATA = BLOCKS + TABLE
SCALE = 1.0 / math.sqrt(SAMPLED * DEVICES)
PARTS = 8
GROUP = 16
BY_LANES = 5
F32 = jnp.float32
BF16 = jnp.bfloat16


def iota(shape, axis):
    return lax.broadcasted_iota(jnp.int32, shape, axis)


def sylvester(rows, columns):
    common = iota((rows, columns), 0) & iota((rows, columns), 1)
    common = common ^ (common >> 4)
    common = common ^ (common >> 2)
    common = common ^ (common >> 1)
    return (1 - 2 * (common & 1)).astype(F32)


def butterflies(values):
    half = 1
    while half < len(values):
        for start in range(0, len(values), 2 * half):
            for i in range(start, start + half):
                a, b = values[i], values[i + half]
                values[i], values[i + half] = a + b, a - b
        half *= 2
    return values


def transform_in_place(ref, places):
    for place, value in zip(places, butterflies([ref[place, :] for place in places])):
        ref[place, :] = value


def aligned(start, size):
    return pl.ds(pl.multiple_of(start, 8), size)


def slot_table(sampled, owners, at_row, named):
    one_hot = iota((DEVICES, SAMPLED), 0) == owners
    one_hot16 = one_hot.astype(F32).astype(BF16)
    upto = iota((SAMPLED, SAMPLED), 0) <= iota((SAMPLED, SAMPLED), 1)
    running = jnp.dot(one_hot16, upto.astype(F32).astype(BF16), preferred_element_type=F32)
    counts = jnp.broadcast_to(running[:, SAMPLED - 1 :], (DEVICES, LANES))
    below = iota((DEVICES, DEVICES), 1) < iota((DEVICES, DEVICES), 0)
    starts = jnp.dot(
        below.astype(F32).astype(BF16), counts.astype(BF16), preferred_element_type=F32
    )
    place = jnp.sum(
        jnp.where(one_hot, running + starts[:, :1], 0.0), axis=0, keepdims=True
    ).astype(jnp.int32) - 1
    at_row[...] = jnp.where(iota((DEVICES, SAMPLED), 0) == place >> 7, 1.0, 0.0)
    at_lane = iota((DEVICES, SAMPLED), 0) == place & (LANES - 1)
    table = jnp.zeros((DEVICES, LANES), F32)
    for part, weight in ((sampled >> 7, 128.0), (sampled & 127, 1.0)):
        named[...] = jnp.where(at_lane, part.astype(F32), 0.0)
        table = table + weight * lax.dot_general(
            at_row[...].astype(BF16),
            named[...].astype(BF16),
            (((1,), (1,)), ((), ())),
            preferred_element_type=F32,
        )
    half = LISTED // 2
    rest = [starts.T[:1], counts.T[:1], jnp.zeros((TABLE - half - 2, LANES), F32)]
    return [
        jnp.concatenate([table[:half]] + rest, axis=0),
        jnp.concatenate([table[half:LISTED]] + rest, axis=0),
    ]


def local_kernel(
    design_hbm, signs_hbm, sampled_hbm, owner_hbm, out_ref,
    design, signs, sampled, owners, at_row, named, mixed, turned, sems, small_sems,
):
    chunk = ROWS // PARTS
    small = [
        pltpu.make_async_copy(source, target, small_sems.at[n])
        for n, (source, target) in enumerate(
            ((sampled_hbm, sampled), (owner_hbm, owners), (signs_hbm, signs))
        )
    ]
    copies = [
        pltpu.make_async_copy(
            design_hbm.at[pl.ds(n * chunk, chunk)], design.at[pl.ds(n * chunk, chunk)], sems.at[n]
        )
        for n in range(PARTS)
    ]
    for copy in small + copies:
        copy.start()
    order = 2 * LANES
    pairs = BLOCKS // 2
    matrix = sylvester(order, order)
    for copy in small:
        copy.wait()
    halves = slot_table(sampled[...], owners[...], at_row, named)
    for n in range(PARTS):
        copies[n].wait()
        for pair in range(n * pairs // PARTS, (n + 1) * pairs // PARTS):
            sign = (2 * signs[2 * pair : 2 * pair + 2, :] - 1).astype(F32)
            signed = jnp.concatenate(
                [matrix[:, :LANES] * sign[0:1], matrix[:, LANES:] * sign[1:2]], axis=1
            ).astype(BF16)
            rows = pl.ds(pair * order, order)
            mixed[rows, :] = jnp.dot(signed, design[rows, :], preferred_element_type=F32)

    @pl.loop(0, order // 8)
    def _(slab):
        transform_in_place(
            mixed, [aligned(pair * order + slab * 8, 8) for pair in range(pairs)]
        )

    for block in range(BLOCKS):
        rows = slice(block * LANES, (block + 1) * LANES)
        turned[rows, :] = mixed[rows, :].T

    @pl.loop(0, COLS // 2, unroll=2)
    def _(pair):
        for t in range(2):
            column = 2 * pair + t
            for part in range(BLOCKS // 8):
                out_ref[aligned(column * DATA + part * 8, 8), :] = turned[
                    pl.ds(part * 8 * COLS + column, 8, stride=COLS), :
                ]
            out_ref[aligned(column * DATA + BLOCKS, TABLE), :] = halves[t]


def gather_rows(parts):
    row = iota((8, LANES), 0)
    step = 1
    while len(parts) > 1:
        upper = (row & step) != 0
        parts = [
            jnp.where(upper, b, a) + pltpu.roll(jnp.where(upper, a, b), step, 0)
            for a, b in zip(parts[0::2], parts[1::2])
        ]
        step *= 2
    return parts[0]


def mix_kernel(column_ref, out_ref):
    @pl.loop(0, BLOCKS, unroll=4)
    def _(step):
        part, low = step // 8, step % 8
        places = [high * 8 + low for high in range(16)]
        values = butterflies(
            [column_ref[aligned(place * DATA + part * 8, 8), :] for place in places]
        )
        for place, value in zip(places, values):
            out_ref[aligned(place * BLOCKS + part * 8, 8), :] = value

    @pl.loop(0, 2 * BLOCKS, unroll=4)
    def _(step):
        part, high = step // 16, step % 16
        transform_in_place(
            out_ref,
            [aligned((high * 8 + low) * BLOCKS + part * 8, 8) for low in range(8)],
        )


def pick_kernel(core_ref, mixed, own_ref, other_ref, out_ref, found, picked):
    first = core_ref[0] == 0
    place = iota((LANES, LANES), 0).astype(F32).astype(BF16)
    row8 = iota((8, LANES), 0)
    one, zero = jnp.ones((), BF16), jnp.zeros((), BF16)

    def samples(source):
        rows = aligned(source * TABLE, TABLE)
        own, other = own_ref[rows, :], other_ref[rows, :]
        lower, upper = jnp.where(first, own, other), jnp.where(first, other, own)
        half = LISTED // 2
        return jnp.concatenate([lower[:half], upper[:half]], axis=0).astype(jnp.int32)

    def pick_by_lanes(source):
        listed = samples(source)
        lane, block = listed & (LANES - 1), listed >> 7

        def choose(low, level):
            if level == 0:
                row = mixed[pl.ds(source * BLOCKS + low, 1), :]
                return jnp.take_along_axis(jnp.broadcast_to(row, (8, LANES)), lane, axis=1)
            a, b = choose(low, level - 1), choose(low + (1 << (level - 1)), level - 1)
            return jnp.where((block >> (level - 1)) & 1 == 1, b, a)

        found[aligned(source * LISTED, LISTED), :] = choose(0, 6)

    def pick_by_matmul(source):
        listed = samples(source)
        key = (listed & (LANES - 1)).astype(F32)
        block = listed >> 7
        values = mixed[aligned(source * BLOCKS, BLOCKS), :]
        top = values.astype(BF16)
        operand = jnp.concatenate([top, (values - top.astype(F32)).astype(BF16)], axis=0)
        parts = []
        for r in range(LISTED):
            mine = jnp.broadcast_to(key[r : r + 1], (16, LANES)).astype(BF16)
            one_hot = jnp.concatenate(
                [jnp.where(place[16 * g : 16 * g + 16] == mine, one, zero) for g in range(8)],
                axis=0,
            )
            result = jnp.dot(operand, one_hot, preferred_element_type=F32)
            wanted = jnp.broadcast_to(block[r : r + 1], (8, LANES))
            values = [
                result[8 * g : 8 * g + 8] + result[BLOCKS + 8 * g : BLOCKS + 8 * g + 8]
                for g in range(8)
            ]
            for n in range(3, 6):
                odd = (wanted >> n) & 1 == 1
                values = [jnp.where(odd, b, a) for a, b in zip(values[0::2], values[1::2])]
            parts.append(jnp.where(wanted & 7 == row8, values[0], 0.0))
        found[aligned(source * LISTED, LISTED), :] = gather_rows(parts)

    def pick(group, n):
        every = GROUP // BY_LANES if BY_LANES else GROUP + 1
        (pick_by_lanes if (n + 1) % every == 0 else pick_by_matmul)(group * GROUP + n)

    def place_in_slots(source):
        spans = own_ref[aligned(source * TABLE, TABLE), :].astype(jnp.int32)
        start, count = (jnp.broadcast_to(spans[n : n + 1], (8, LANES)) for n in (4, 5))
        here = found[aligned(source * LISTED, LISTED), :]
        for t in range(2):
            position = row8 + 8 * t
            slot = start + position
            lane = slot & (LANES - 1)
            rows = [
                jnp.take_along_axis(jnp.broadcast_to(here[r : r + 1], (8, LANES)), lane, axis=1)
                for r in range(LISTED)
            ]
            for n in range(3):
                odd = (slot >> (7 + n)) & 1 == 1
                rows = [jnp.where(odd, b, a) for a, b in zip(rows[0::2], rows[1::2])]
            picked[aligned(source * CAP + 8 * t, 8), :] = jnp.where(
                position < count, rows[0] * SCALE, 0.0
            )

    for n in range(GROUP):
        pick(0, n)

    @pl.loop(1, DEVICES // GROUP)
    def _(group):
        for n in range(GROUP):
            place_in_slots((group - 1) * GROUP + n)
            pick(group, n)

    for n in range(GROUP):
        place_in_slots(DEVICES - GROUP + n)

    for group in range(CAP):
        out_ref[pl.ds(group, DEVICES, stride=CAP), :] = picked[
            group * LANES : (group + 1) * LANES, :
        ].T


def turn_kernel(arrived_ref, out_ref):
    for group in range(CAP):
        out_ref[group * LANES : (group + 1) * LANES, :] = arrived_ref[
            pl.ds(group, COLS, stride=CAP), :
        ].T


HBM = pl.BlockSpec(memory_space=pltpu.HBM)
VMEM = pl.BlockSpec(memory_space=pltpu.VMEM)
SMEM = pl.BlockSpec(memory_space=pltpu.SMEM)


def call(kernel, rows, specs, *args, scratch=(), limit=24):
    shapes = [jax.ShapeDtypeStruct((n, LANES), F32) for n in rows]
    return pl.pallas_call(
        kernel,
        out_shape=shapes,
        in_specs=specs,
        out_specs=[VMEM] * len(rows),
        scratch_shapes=scratch,
        compiler_params=pltpu.CompilerParams(vmem_limit_bytes=limit * 1024 * 1024),
    )(*args)


def local_call(design, sign_bits, sampled, owner_map):
    vmem, dma = pltpu.VMEM, pltpu.SemaphoreType.DMA
    return call(
        local_kernel,
        [COLS * DATA],
        [HBM] * 4,
        design,
        sign_bits.reshape(BLOCKS, LANES),
        sampled.reshape(1, SAMPLED),
        owner_map.reshape(1, SAMPLED),
        scratch=[
            vmem((ROWS, LANES), BF16),
            vmem((BLOCKS, LANES), jnp.int32),
            vmem((1, SAMPLED), jnp.int32),
            vmem((1, SAMPLED), jnp.int32),
            vmem((DEVICES, SAMPLED), F32),
            vmem((DEVICES, SAMPLED), F32),
            vmem((ROWS, LANES), F32),
            vmem((ROWS, LANES), F32),
            dma((PARTS,)),
            dma((3,)),
        ],
    )[0]


def mix_call(columns):
    return call(mix_kernel, [DEVICES * BLOCKS], [VMEM], columns)[0]


def pick_call(core, mixed, own, other):
    return call(
        pick_kernel,
        [DEVICES * CAP],
        [SMEM, VMEM, VMEM, VMEM],
        core,
        mixed,
        own,
        other,
        scratch=[
            pltpu.VMEM((DEVICES * LISTED, LANES), F32),
            pltpu.VMEM((DEVICES * CAP, LANES), F32),
        ],
    )[0]


def exchange(values):
    values = values.reshape(DEVICES, 1, -1)
    return lax.all_to_all(values, AXES, split_axis=0, concat_axis=0, tiled=True).reshape(
        -1, LANES
    )


def per_device(design, sign_bits, sampled, owner_map):
    columns = exchange(local_call(design, sign_bits, sampled, owner_map))
    own = columns.reshape(DEVICES, DATA, LANES)[:, BLOCKS:].reshape(-1, LANES)
    cores = [(place, place ^ 1) for place in range(lax.axis_size("outer"))]
    other = lax.ppermute(own, "outer", cores)
    core = (lax.axis_index("outer") & 1).astype(jnp.int32).reshape(1)
    picked = exchange(pick_call(core, mix_call(columns), own, other))
    (tiles,) = call(turn_kernel, [DEVICES * CAP], [VMEM], picked)
    return tiles.reshape(1, DEVICES, CAP, COLS)


def solution(mesh):
    in_specs = (
        P(AXES, None),
        P(AXES),
        P(AXES),
        P(AXES, None),
    )
    out_specs = P(AXES, None, None, None)
    return jax.shard_map(
        per_device, mesh=mesh, in_specs=in_specs, out_specs=out_specs, check_vma=False
    )
```

```python
import math

import jax
import jax.numpy as jnp
from jax import lax
from jax.experimental import pallas as pl
from jax.experimental.pallas import tpu as pltpu
from jax.sharding import PartitionSpec as P

AXES = ("inner", "outer")
DEVICES = 128
COLS = 128
LANES = 128
BLOCKS = 64
ROWS = BLOCKS * LANES
SAMPLED = 1024
CAP = 16
LISTED = SAMPLED // LANES
TABLE = 8
DATA = BLOCKS + TABLE
SCALE = 1.0 / math.sqrt(SAMPLED * DEVICES)
PARTS = 8
GROUP = 16
BY_LANES = 5
F32 = jnp.float32
BF16 = jnp.bfloat16


def iota(shape, axis):
    return lax.broadcasted_iota(jnp.int32, shape, axis)


def sylvester(rows, columns):
    common = iota((rows, columns), 0) & iota((rows, columns), 1)
    common = common ^ (common >> 4)
    common = common ^ (common >> 2)
    common = common ^ (common >> 1)
    return (1 - 2 * (common & 1)).astype(F32)


def butterflies(values):
    half = 1
    while half < len(values):
        for start in range(0, len(values), 2 * half):
            for i in range(start, start + half):
                a, b = values[i], values[i + half]
                values[i], values[i + half] = a + b, a - b
        half *= 2
    return values


def transform_in_place(ref, places):
    for place, value in zip(places, butterflies([ref[place, :] for place in places])):
        ref[place, :] = value


def aligned(start, size):
    return pl.ds(pl.multiple_of(start, 8), size)


def slot_table(sampled, owners, at_row, named):
    one_hot = iota((DEVICES, SAMPLED), 0) == owners
    one_hot16 = one_hot.astype(F32).astype(BF16)
    upto = iota((SAMPLED, SAMPLED), 0) <= iota((SAMPLED, SAMPLED), 1)
    running = jnp.dot(one_hot16, upto.astype(F32).astype(BF16), preferred_element_type=F32)
    counts = jnp.broadcast_to(running[:, SAMPLED - 1 :], (DEVICES, LANES))
    below = iota((DEVICES, DEVICES), 1) < iota((DEVICES, DEVICES), 0)
    starts = jnp.dot(
        below.astype(F32).astype(BF16), counts.astype(BF16), preferred_element_type=F32
    )
    place = jnp.sum(
        jnp.where(one_hot, running + starts[:, :1], 0.0), axis=0, keepdims=True
    ).astype(jnp.int32) - 1
    at_row[...] = jnp.where(iota((DEVICES, SAMPLED), 0) == place >> 7, 1.0, 0.0)
    at_lane = iota((DEVICES, SAMPLED), 0) == place & (LANES - 1)
    table = jnp.zeros((DEVICES, LANES), F32)
    block = ((sampled >> 7 & 1) << 5) + (sampled >> 8)
    for part, weight in ((block, 128.0), (sampled & 127, 1.0)):
        named[...] = jnp.where(at_lane, part.astype(F32), 0.0)
        table = table + weight * lax.dot_general(
            at_row[...].astype(BF16),
            named[...].astype(BF16),
            (((1,), (1,)), ((), ())),
            preferred_element_type=F32,
        )
    half = LISTED // 2
    rest = [starts.T[:1], counts.T[:1], jnp.zeros((TABLE - half - 2, LANES), F32)]
    return [
        jnp.concatenate([table[:half]] + rest, axis=0),
        jnp.concatenate([table[half:LISTED]] + rest, axis=0),
    ]


def local_kernel(
    design_hbm, signs_hbm, sampled_hbm, owner_hbm, out_hbm,
    design, signs, sampled, owners, at_row, named, mixed, turned, out, sems, small_sems, out_sems,
):
    chunk = ROWS // PARTS
    small = [
        pltpu.make_async_copy(source, target, small_sems.at[n])
        for n, (source, target) in enumerate(
            ((sampled_hbm, sampled), (owner_hbm, owners), (signs_hbm, signs))
        )
    ]
    copies = [
        pltpu.make_async_copy(
            design_hbm.at[pl.ds(n * chunk, chunk)], design.at[pl.ds(n * chunk, chunk)], sems.at[n]
        )
        for n in range(PARTS)
    ]
    for copy in small + copies:
        copy.start()
    order = 2 * LANES
    pairs = BLOCKS // 2
    matrix = sylvester(order, order)
    for copy in small:
        copy.wait()
    halves = slot_table(sampled[...], owners[...], at_row, named)
    for n in range(PARTS):
        copies[n].wait()
        for pair in range(n * pairs // PARTS, (n + 1) * pairs // PARTS):
            sign = (2 * signs[2 * pair : 2 * pair + 2, :] - 1).astype(F32)
            signed = jnp.concatenate(
                [matrix[:, :LANES] * sign[0:1], matrix[:, LANES:] * sign[1:2]], axis=1
            ).astype(BF16)
            rows = pl.ds(pair * order, order)
            mixed[rows, :] = jnp.dot(signed, design[rows, :], preferred_element_type=F32)

    @pl.loop(0, order // 8)
    def _(slab):
        transform_in_place(
            mixed, [aligned(pair * order + slab * 8, 8) for pair in range(pairs)]
        )

    for t in range(2):
        for pair in range(pairs):
            place = t * pairs + pair
            turned[place * LANES : (place + 1) * LANES, :] = mixed[
                (2 * pair + t) * LANES : (2 * pair + t + 1) * LANES, :
            ].T

    columns = COLS // PARTS

    def send(step):
        rows = aligned(step * columns * DATA, columns * DATA)
        return pltpu.make_async_copy(out.at[rows], out_hbm.at[rows], out_sems.at[step])

    @pl.loop(0, PARTS)
    def _(step):
        for part in range(BLOCKS // 8):
            for first in range(0, columns, 8):
                tile = jnp.stack(
                    [
                        turned[aligned((part * 8 + n) * COLS + step * columns + first, 8), :]
                        for n in range(8)
                    ]
                )
                tile = jnp.swapaxes(tile, 0, 1)
                for n in range(8):
                    place = (step * columns + first + n) * DATA + part * 8
                    out[aligned(place, 8), :] = tile[n]
        for n in range(columns):
            place = (step * columns + n) * DATA + BLOCKS
            out[aligned(place, TABLE), :] = halves[n % 2]
        send(step).start()

    @pl.loop(0, PARTS)
    def _(step):
        send(step).wait()


def gather_rows(parts):
    row = iota((8, LANES), 0)
    step = 1
    while len(parts) > 1:
        upper = (row & step) != 0
        parts = [
            jnp.where(upper, b, a) + pltpu.roll(jnp.where(upper, a, b), step, 0)
            for a, b in zip(parts[0::2], parts[1::2])
        ]
        step *= 2
    return parts[0]


def mix_kernel(column_ref, out_ref):
    @pl.loop(0, BLOCKS, unroll=4)
    def _(step):
        part, low = step // 8, step % 8
        places = [high * 8 + low for high in range(16)]
        values = butterflies(
            [column_ref[aligned(place * DATA + part * 8, 8), :] for place in places]
        )
        for place, value in zip(places, values):
            out_ref[aligned(place * BLOCKS + part * 8, 8), :] = value

    @pl.loop(0, 2 * BLOCKS, unroll=4)
    def _(step):
        part, high = step // 16, step % 16
        transform_in_place(
            out_ref,
            [aligned((high * 8 + low) * BLOCKS + part * 8, 8) for low in range(8)],
        )


def pick_kernel(mixed, own_ref, other_ref, out_ref, found, picked):
    first = lax.axis_index("outer") % 2 == 0
    place = iota((LANES, LANES), 0).astype(F32).astype(BF16)
    row8 = iota((8, LANES), 0)
    one, zero = jnp.ones((), BF16), jnp.zeros((), BF16)

    def samples(source):
        rows = aligned(source * TABLE, TABLE)
        own, other = own_ref[rows, :], other_ref[rows, :]
        lower, upper = jnp.where(first, own, other), jnp.where(first, other, own)
        half = LISTED // 2
        return jnp.concatenate([lower[:half], upper[:half]], axis=0).astype(jnp.int32)

    def pick_by_lanes(source):
        listed = samples(source)
        lane, block = listed & (LANES - 1), listed >> 7

        def choose(low, level):
            if level == 0:
                row = mixed[pl.ds(source * BLOCKS + low, 1), :]
                return jnp.take_along_axis(jnp.broadcast_to(row, (8, LANES)), lane, axis=1)
            a, b = choose(low, level - 1), choose(low + (1 << (level - 1)), level - 1)
            return jnp.where((block >> (level - 1)) & 1 == 1, b, a)

        found[aligned(source * LISTED, LISTED), :] = choose(0, 6)

    def pick_by_matmul(source):
        listed = samples(source)
        key = (listed & (LANES - 1)).astype(F32)
        block = listed >> 7
        values = mixed[aligned(source * BLOCKS, BLOCKS), :]
        top = values.astype(BF16)
        operand = jnp.concatenate([top, (values - top.astype(F32)).astype(BF16)], axis=0)
        parts = []
        for r in range(LISTED):
            mine = jnp.broadcast_to(key[r : r + 1], (16, LANES)).astype(BF16)
            one_hot = jnp.concatenate(
                [jnp.where(place[16 * g : 16 * g + 16] == mine, one, zero) for g in range(8)],
                axis=0,
            )
            result = jnp.dot(operand, one_hot, preferred_element_type=F32)
            wanted = jnp.broadcast_to(block[r : r + 1], (8, LANES))
            values = [
                result[8 * g : 8 * g + 8] + result[BLOCKS + 8 * g : BLOCKS + 8 * g + 8]
                for g in range(8)
            ]
            for n in range(3, 6):
                odd = (wanted >> n) & 1 == 1
                values = [jnp.where(odd, b, a) for a, b in zip(values[0::2], values[1::2])]
            parts.append(jnp.where(wanted & 7 == row8, values[0], 0.0))
        found[aligned(source * LISTED, LISTED), :] = gather_rows(parts)

    def pick(group, n):
        every = GROUP // BY_LANES if BY_LANES else GROUP + 1
        (pick_by_lanes if (n + 1) % every == 0 else pick_by_matmul)(group * GROUP + n)

    def place_in_slots(source):
        spans = own_ref[aligned(source * TABLE, TABLE), :].astype(jnp.int32)
        start, count = (jnp.broadcast_to(spans[n : n + 1], (8, LANES)) for n in (4, 5))
        here = found[aligned(source * LISTED, LISTED), :]
        for t in range(2):
            position = row8 + 8 * t
            slot = start + position
            lane = slot & (LANES - 1)
            rows = [
                jnp.take_along_axis(jnp.broadcast_to(here[r : r + 1], (8, LANES)), lane, axis=1)
                for r in range(LISTED)
            ]
            for n in range(3):
                odd = (slot >> (7 + n)) & 1 == 1
                rows = [jnp.where(odd, b, a) for a, b in zip(rows[0::2], rows[1::2])]
            picked[aligned(source * CAP + 8 * t, 8), :] = jnp.where(
                position < count, rows[0] * SCALE, 0.0
            )

    for n in range(GROUP):
        pick(0, n)

    @pl.loop(1, DEVICES // GROUP)
    def _(group):
        for n in range(GROUP):
            place_in_slots((group - 1) * GROUP + n)
            pick(group, n)

    for n in range(GROUP):
        place_in_slots(DEVICES - GROUP + n)

    for group in range(CAP):
        out_ref[pl.ds(group, DEVICES, stride=CAP), :] = picked[
            group * LANES : (group + 1) * LANES, :
        ].T


def turn_kernel(arrived_ref, out_ref):
    for group in range(CAP):
        out_ref[group * LANES : (group + 1) * LANES, :] = arrived_ref[
            pl.ds(group, COLS, stride=CAP), :
        ].T


HBM = pl.BlockSpec(memory_space=pltpu.HBM)
VMEM = pl.BlockSpec(memory_space=pltpu.VMEM)


def call(kernel, rows, specs, *args, scratch=(), limit=24, out=VMEM):
    shapes = [jax.ShapeDtypeStruct((n, LANES), F32) for n in rows]
    return pl.pallas_call(
        kernel,
        out_shape=shapes,
        in_specs=specs,
        out_specs=[out] * len(rows),
        scratch_shapes=scratch,
        compiler_params=pltpu.CompilerParams(vmem_limit_bytes=limit * 1024 * 1024),
    )(*args)


def local_call(design, sign_bits, sampled, owner_map):
    vmem, dma = pltpu.VMEM, pltpu.SemaphoreType.DMA
    return call(
        local_kernel,
        [COLS * DATA],
        [HBM] * 4,
        design,
        sign_bits.reshape(BLOCKS, LANES),
        sampled.reshape(1, SAMPLED),
        owner_map.reshape(1, SAMPLED),
        scratch=[
            vmem((ROWS, LANES), BF16),
            vmem((BLOCKS, LANES), jnp.int32),
            vmem((1, SAMPLED), jnp.int32),
            vmem((1, SAMPLED), jnp.int32),
            vmem((DEVICES, SAMPLED), F32),
            vmem((DEVICES, SAMPLED), F32),
            vmem((ROWS, LANES), F32),
            vmem((ROWS, LANES), F32),
            vmem((COLS * DATA, LANES), F32),
            dma((PARTS,)),
            dma((3,)),
            dma((PARTS,)),
        ],
        limit=60,
        out=HBM,
    )[0]


def mix_call(columns):
    return call(mix_kernel, [DEVICES * BLOCKS], [VMEM], columns)[0]


def pick_call(mixed, own, other):
    return call(
        pick_kernel,
        [DEVICES * CAP],
        [VMEM, VMEM, VMEM],
        mixed,
        own,
        other,
        scratch=[
            pltpu.VMEM((DEVICES * LISTED, LANES), F32),
            pltpu.VMEM((DEVICES * CAP, LANES), F32),
        ],
    )[0]


def exchange(values):
    values = values.reshape(DEVICES, 1, -1)
    return lax.all_to_all(values, AXES, split_axis=0, concat_axis=0, tiled=True).reshape(
        -1, LANES
    )


def per_device(design, sign_bits, sampled, owner_map):
    columns = exchange(local_call(design, sign_bits, sampled, owner_map))
    own = columns.reshape(DEVICES, DATA, LANES)[:, BLOCKS:].reshape(-1, LANES)
    cores = [(place, place ^ 1) for place in range(lax.axis_size("outer"))]
    other = lax.ppermute(own, "outer", cores)
    picked = exchange(pick_call(mix_call(columns), own, other))
    (tiles,) = call(turn_kernel, [DEVICES * CAP], [VMEM], picked)
    return tiles.reshape(1, DEVICES, CAP, COLS)


def solution(mesh):
    in_specs = (
        P(AXES, None),
        P(AXES),
        P(AXES),
        P(AXES, None),
    )
    out_specs = P(AXES, None, None, None)
    return jax.shard_map(
        per_device, mesh=mesh, in_specs=in_specs, out_specs=out_specs, check_vma=False
    )
```

```python
import math

import jax
import jax.numpy as jnp
from jax import lax
from jax.experimental import pallas as pl
from jax.experimental.pallas import tpu as pltpu
from jax.sharding import PartitionSpec as P

AXES = ("y", "h", "z", "l", "c")
SIZES = (4, 2, 4, 2, 2)
ORDER = ("y", "z", "h", "l", "c")
DEVICES = 128
COLS = 128
LANES = 128
BLOCKS = 64
ROWS = BLOCKS * LANES
SAMPLED = 1024
CAP = 16
LISTED = SAMPLED // LANES
TABLE = 8
DATA = BLOCKS + TABLE
SCALE = 1.0 / math.sqrt(SAMPLED * DEVICES)
PARTS = 8
GROUP = 16
BY_LANES = 5
F32 = jnp.float32
BF16 = jnp.bfloat16


def iota(shape, axis):
    return lax.broadcasted_iota(jnp.int32, shape, axis)


def sylvester(rows, columns):
    common = iota((rows, columns), 0) & iota((rows, columns), 1)
    common = common ^ (common >> 4)
    common = common ^ (common >> 2)
    common = common ^ (common >> 1)
    return (1 - 2 * (common & 1)).astype(F32)


def butterflies(values):
    half = 1
    while half < len(values):
        for start in range(0, len(values), 2 * half):
            for i in range(start, start + half):
                a, b = values[i], values[i + half]
                values[i], values[i + half] = a + b, a - b
        half *= 2
    return values


def transform_in_place(ref, places):
    for place, value in zip(places, butterflies([ref[place, :] for place in places])):
        ref[place, :] = value


def aligned(start, size):
    return pl.ds(pl.multiple_of(start, 8), size)


def rank_of(place):
    return (place & 99) + ((place >> 2 & 3) << 3) + ((place >> 4 & 1) << 2)


def place_of(rank):
    return (rank & 99) + ((rank >> 3 & 3) << 2) + ((rank >> 2 & 1) << 4)


def slot_table(sampled, owners, at_row, named):
    one_hot = iota((DEVICES, SAMPLED), 0) == rank_of(owners)
    one_hot16 = one_hot.astype(F32).astype(BF16)
    upto = iota((SAMPLED, SAMPLED), 0) <= iota((SAMPLED, SAMPLED), 1)
    running = jnp.dot(one_hot16, upto.astype(F32).astype(BF16), preferred_element_type=F32)
    counts = jnp.broadcast_to(running[:, SAMPLED - 1 :], (DEVICES, LANES))
    below = iota((DEVICES, DEVICES), 1) < iota((DEVICES, DEVICES), 0)
    starts = jnp.dot(
        below.astype(F32).astype(BF16), counts.astype(BF16), preferred_element_type=F32
    )
    place = jnp.sum(
        jnp.where(one_hot, running + starts[:, :1], 0.0), axis=0, keepdims=True
    ).astype(jnp.int32) - 1
    at_row[...] = jnp.where(iota((DEVICES, SAMPLED), 0) == place >> 7, 1.0, 0.0)
    at_lane = iota((DEVICES, SAMPLED), 0) == place & (LANES - 1)
    table = jnp.zeros((DEVICES, LANES), F32)
    block = ((sampled >> 7 & 1) << 5) + (sampled >> 8)
    for part, weight in ((block, 128.0), (sampled & 127, 1.0)):
        named[...] = jnp.where(at_lane, part.astype(F32), 0.0)
        table = table + weight * lax.dot_general(
            at_row[...].astype(BF16),
            named[...].astype(BF16),
            (((1,), (1,)), ((), ())),
            preferred_element_type=F32,
        )
    half = LISTED // 2
    rest = [starts.T[:1], counts.T[:1], jnp.zeros((TABLE - half - 2, LANES), F32)]
    return [
        jnp.concatenate([table[:half]] + rest, axis=0),
        jnp.concatenate([table[half:LISTED]] + rest, axis=0),
    ]


def local_kernel(
    design_hbm, signs_hbm, sampled_hbm, owner_hbm, out_hbm,
    design, signs, sampled, owners, at_row, named, mixed, turned, out, sems, small_sems, out_sems,
):
    chunk = ROWS // PARTS
    small = [
        pltpu.make_async_copy(source, target, small_sems.at[n])
        for n, (source, target) in enumerate(
            ((sampled_hbm, sampled), (owner_hbm, owners), (signs_hbm, signs))
        )
    ]
    copies = [
        pltpu.make_async_copy(
            design_hbm.at[pl.ds(n * chunk, chunk)], design.at[pl.ds(n * chunk, chunk)], sems.at[n]
        )
        for n in range(PARTS)
    ]
    for copy in small + copies:
        copy.start()
    order = 2 * LANES
    pairs = BLOCKS // 2
    matrix = sylvester(order, order)
    for copy in small:
        copy.wait()
    halves = slot_table(sampled[...], owners[...], at_row, named)
    for n in range(PARTS):
        copies[n].wait()
        for pair in range(n * pairs // PARTS, (n + 1) * pairs // PARTS):
            sign = (2 * signs[2 * pair : 2 * pair + 2, :] - 1).astype(F32)
            signed = jnp.concatenate(
                [matrix[:, :LANES] * sign[0:1], matrix[:, LANES:] * sign[1:2]], axis=1
            ).astype(BF16)
            rows = pl.ds(pair * order, order)
            mixed[rows, :] = jnp.dot(signed, design[rows, :], preferred_element_type=F32)

    @pl.loop(0, order // 8, unroll=2)
    def _(slab):
        transform_in_place(
            mixed, [aligned(pair * order + slab * 8, 8) for pair in range(pairs)]
        )

    for t in range(2):
        for pair in range(pairs):
            place = t * pairs + pair
            turned[place * LANES : (place + 1) * LANES, :] = mixed[
                (2 * pair + t) * LANES : (2 * pair + t + 1) * LANES, :
            ].T

    columns = COLS // PARTS

    def send(step):
        rows = aligned(step * columns * DATA, columns * DATA)
        return pltpu.make_async_copy(out.at[rows], out_hbm.at[rows], out_sems.at[step])

    @pl.loop(0, PARTS)
    def _(step):
        for part in range(BLOCKS // 8):
            for first in range(0, columns, 8):
                tile = jnp.stack(
                    [
                        turned[aligned((part * 8 + n) * COLS + step * columns + first, 8), :]
                        for n in range(8)
                    ]
                )
                tile = jnp.swapaxes(tile, 0, 1)
                for n in range(8):
                    place = (step * columns + first + n) * DATA + part * 8
                    out[aligned(place, 8), :] = tile[n]
        for n in range(columns):
            place = (step * columns + n) * DATA + BLOCKS
            out[aligned(place, TABLE), :] = halves[n % 2]
        send(step).start()

    @pl.loop(0, PARTS)
    def _(step):
        send(step).wait()


def gather_rows(parts):
    row = iota((8, LANES), 0)
    step = 1
    while len(parts) > 1:
        upper = (row & step) != 0
        parts = [
            jnp.where(upper, b, a) + pltpu.roll(jnp.where(upper, a, b), step, 0)
            for a, b in zip(parts[0::2], parts[1::2])
        ]
        step *= 2
    return parts[0]


def mix_kernel(column_ref, out_ref):
    @pl.loop(0, BLOCKS, unroll=4)
    def _(step):
        part, low = step // 8, step % 8
        places = [high * 8 + low for high in range(16)]
        values = butterflies(
            [column_ref[aligned(place * DATA + part * 8, 8), :] for place in places]
        )
        for place, value in zip(places, values):
            out_ref[aligned(place * BLOCKS + part * 8, 8), :] = value

    @pl.loop(0, 2 * BLOCKS, unroll=4)
    def _(step):
        part, high = step // 16, step % 16
        transform_in_place(
            out_ref,
            [aligned((high * 8 + low) * BLOCKS + part * 8, 8) for low in range(8)],
        )


def pick_kernel(mixed, own_ref, other_ref, out_ref, found, picked):
    first = lax.axis_index("c") == 0
    place = iota((LANES, LANES), 0).astype(F32).astype(BF16)
    row8 = iota((8, LANES), 0)
    one, zero = jnp.ones((), BF16), jnp.zeros((), BF16)

    def samples(source):
        rows = aligned(source * TABLE, TABLE)
        own, other = own_ref[rows, :], other_ref[rows, :]
        lower, upper = jnp.where(first, own, other), jnp.where(first, other, own)
        half = LISTED // 2
        return jnp.concatenate([lower[:half], upper[:half]], axis=0).astype(jnp.int32)

    def pick_by_lanes(source):
        listed = samples(source)
        lane, block = listed & (LANES - 1), listed >> 7

        def choose(low, level):
            if level == 0:
                row = mixed[pl.ds(source * BLOCKS + low, 1), :]
                return jnp.take_along_axis(jnp.broadcast_to(row, (8, LANES)), lane, axis=1)
            a, b = choose(low, level - 1), choose(low + (1 << (level - 1)), level - 1)
            return jnp.where((block >> (level - 1)) & 1 == 1, b, a)

        found[aligned(source * LISTED, LISTED), :] = choose(0, 6)

    def pick_by_matmul(source):
        listed = samples(source)
        key = (listed & (LANES - 1)).astype(F32)
        block = listed >> 7
        values = mixed[aligned(source * BLOCKS, BLOCKS), :]
        top = values.astype(BF16)
        operand = jnp.concatenate([top, (values - top.astype(F32)).astype(BF16)], axis=0)
        parts = []
        for r in range(LISTED):
            mine = jnp.broadcast_to(key[r : r + 1], (16, LANES)).astype(BF16)
            one_hot = jnp.concatenate(
                [jnp.where(place[16 * g : 16 * g + 16] == mine, one, zero) for g in range(8)],
                axis=0,
            )
            result = jnp.dot(operand, one_hot, preferred_element_type=F32)
            wanted = jnp.broadcast_to(block[r : r + 1], (8, LANES))
            values = [
                result[8 * g : 8 * g + 8] + result[BLOCKS + 8 * g : BLOCKS + 8 * g + 8]
                for g in range(8)
            ]
            for n in range(3, 6):
                odd = (wanted >> n) & 1 == 1
                values = [jnp.where(odd, b, a) for a, b in zip(values[0::2], values[1::2])]
            parts.append(jnp.where(wanted & 7 == row8, values[0], 0.0))
        found[aligned(source * LISTED, LISTED), :] = gather_rows(parts)

    def pick(group, n):
        every = GROUP // BY_LANES if BY_LANES else GROUP + 1
        (pick_by_lanes if (n + 1) % every == 0 else pick_by_matmul)(group * GROUP + n)

    def place_in_slots(source):
        spans = own_ref[aligned(source * TABLE, TABLE), :].astype(jnp.int32)
        start, count = (jnp.broadcast_to(spans[n : n + 1], (8, LANES)) for n in (4, 5))
        here = found[aligned(source * LISTED, LISTED), :]
        for t in range(2):
            position = row8 + 8 * t
            slot = start + position
            lane = slot & (LANES - 1)
            rows = [
                jnp.take_along_axis(jnp.broadcast_to(here[r : r + 1], (8, LANES)), lane, axis=1)
                for r in range(LISTED)
            ]
            for n in range(3):
                odd = (slot >> (7 + n)) & 1 == 1
                rows = [jnp.where(odd, b, a) for a, b in zip(rows[0::2], rows[1::2])]
            picked[aligned(place_of(source) * CAP + 8 * t, 8), :] = jnp.where(
                position < count, rows[0] * SCALE, 0.0
            )

    for n in range(GROUP):
        pick(0, n)

    @pl.loop(1, DEVICES // GROUP)
    def _(group):
        for n in range(GROUP):
            place_in_slots((group - 1) * GROUP + n)
            pick(group, n)

    for n in range(GROUP):
        place_in_slots(DEVICES - GROUP + n)

    for group in range(CAP):
        out_ref[pl.ds(group, DEVICES, stride=CAP), :] = picked[
            group * LANES : (group + 1) * LANES, :
        ].T


def turn_kernel(arrived_ref, out_ref):
    for group in range(CAP):
        out_ref[group * LANES : (group + 1) * LANES, :] = arrived_ref[
            pl.ds(group, COLS, stride=CAP), :
        ].T


HBM = pl.BlockSpec(memory_space=pltpu.HBM)
VMEM = pl.BlockSpec(memory_space=pltpu.VMEM)


def call(kernel, rows, specs, *args, scratch=(), limit=24, out=VMEM):
    shapes = [jax.ShapeDtypeStruct((n, LANES), F32) for n in rows]
    return pl.pallas_call(
        kernel,
        out_shape=shapes,
        in_specs=specs,
        out_specs=[out] * len(rows),
        scratch_shapes=scratch,
        compiler_params=pltpu.CompilerParams(vmem_limit_bytes=limit * 1024 * 1024),
    )(*args)


def local_call(design, sign_bits, sampled, owner_map):
    vmem, dma = pltpu.VMEM, pltpu.SemaphoreType.DMA
    return call(
        local_kernel,
        [COLS * DATA],
        [HBM] * 4,
        design,
        sign_bits.reshape(BLOCKS, LANES),
        sampled.reshape(1, SAMPLED),
        owner_map.reshape(1, SAMPLED),
        scratch=[
            vmem((ROWS, LANES), BF16),
            vmem((BLOCKS, LANES), jnp.int32),
            vmem((1, SAMPLED), jnp.int32),
            vmem((1, SAMPLED), jnp.int32),
            vmem((DEVICES, SAMPLED), F32),
            vmem((DEVICES, SAMPLED), F32),
            vmem((ROWS, LANES), F32),
            vmem((ROWS, LANES), F32),
            vmem((COLS * DATA, LANES), F32),
            dma((PARTS,)),
            dma((3,)),
            dma((PARTS,)),
        ],
        limit=60,
        out=HBM,
    )[0]


def mix_call(columns):
    return call(mix_kernel, [DEVICES * BLOCKS], [VMEM], columns)[0]


def pick_call(mixed, own, other):
    return call(
        pick_kernel,
        [DEVICES * CAP],
        [VMEM, VMEM, VMEM],
        mixed,
        own,
        other,
        scratch=[
            pltpu.VMEM((DEVICES * LISTED, LANES), F32),
            pltpu.VMEM((DEVICES * CAP, LANES), F32),
        ],
    )[0]


def exchange(values):
    values = values.reshape(DEVICES, 1, -1)
    return lax.all_to_all(values, ORDER, split_axis=0, concat_axis=0, tiled=True).reshape(
        -1, LANES
    )


def per_device(design, sign_bits, sampled, owner_map):
    columns = exchange(local_call(design, sign_bits, sampled, owner_map))
    own = columns.reshape(DEVICES, DATA, LANES)[:, BLOCKS:].reshape(-1, LANES)
    other = lax.ppermute(own, "c", [(0, 1), (1, 0)])
    picked = exchange(pick_call(mix_call(columns), own, other))
    (tiles,) = call(turn_kernel, [DEVICES * CAP], [VMEM], picked)
    return tiles.reshape(1, DEVICES, CAP, COLS)


def solution(mesh):
    in_specs = (
        P(AXES, None),
        P(AXES),
        P(AXES),
        P(AXES, None),
    )
    out_specs = P(AXES, None, None, None)
    fine = jax.sharding.Mesh(mesh.devices.reshape(SIZES), AXES)
    return jax.shard_map(
        per_device, mesh=fine, in_specs=in_specs, out_specs=out_specs, check_vma=False
    )
```

```python
import math

import jax
import jax.numpy as jnp
from jax import lax
from jax.experimental import pallas as pl
from jax.experimental.pallas import tpu as pltpu
from jax.sharding import PartitionSpec as P

AXES = ("y", "h", "z", "l", "c")
SIZES = (4, 2, 4, 2, 2)
ORDER = ("y", "z", "h", "l", "c")
DEVICES = 128
COLS = 128
LANES = 128
BLOCKS = 64
ROWS = BLOCKS * LANES
SAMPLED = 1024
CAP = 16
LISTED = SAMPLED // LANES
TABLE = 8
DATA = BLOCKS + TABLE
SCALE = 1.0 / math.sqrt(SAMPLED * DEVICES)
PARTS = 8
GROUP = 64
BY_LANES = 21
F32 = jnp.float32
BF16 = jnp.bfloat16


def iota(shape, axis):
    return lax.broadcasted_iota(jnp.int32, shape, axis)


def sylvester(rows, columns):
    common = iota((rows, columns), 0) & iota((rows, columns), 1)
    common = common ^ (common >> 4)
    common = common ^ (common >> 2)
    common = common ^ (common >> 1)
    return (1 - 2 * (common & 1)).astype(F32)


def butterflies(values):
    half = 1
    while half < len(values):
        for start in range(0, len(values), 2 * half):
            for i in range(start, start + half):
                a, b = values[i], values[i + half]
                values[i], values[i + half] = a + b, a - b
        half *= 2
    return values


def transform_in_place(ref, places):
    for place, value in zip(places, butterflies([ref[place, :] for place in places])):
        ref[place, :] = value


def aligned(start, size):
    return pl.ds(pl.multiple_of(start, 8), size)


def rank_of(place):
    return (place & 99) + ((place >> 2 & 3) << 3) + ((place >> 4 & 1) << 2)


def place_of(rank):
    return (rank & 99) + ((rank >> 3 & 3) << 2) + ((rank >> 2 & 1) << 4)


def slot_table(sampled, owners, at_row, named):
    one_hot = iota((DEVICES, SAMPLED), 0) == rank_of(owners)
    one_hot16 = one_hot.astype(F32).astype(BF16)
    upto = iota((SAMPLED, SAMPLED), 0) <= iota((SAMPLED, SAMPLED), 1)
    running = jnp.dot(one_hot16, upto.astype(F32).astype(BF16), preferred_element_type=F32)
    counts = jnp.broadcast_to(running[:, SAMPLED - 1 :], (DEVICES, LANES))
    below = iota((DEVICES, DEVICES), 1) < iota((DEVICES, DEVICES), 0)
    starts = jnp.dot(
        below.astype(F32).astype(BF16), counts.astype(BF16), preferred_element_type=F32
    )
    place = jnp.sum(
        jnp.where(one_hot, running + starts[:, :1], 0.0), axis=0, keepdims=True
    ).astype(jnp.int32) - 1
    at_row[...] = jnp.where(iota((DEVICES, SAMPLED), 0) == place >> 7, 1.0, 0.0)
    at_lane = iota((DEVICES, SAMPLED), 0) == place & (LANES - 1)
    table = jnp.zeros((DEVICES, LANES), F32)
    block = ((sampled >> 7 & 1) << 5) + (sampled >> 8)
    for part, weight in ((block, 128.0), (sampled & 127, 1.0)):
        named[...] = jnp.where(at_lane, part.astype(F32), 0.0)
        table = table + weight * lax.dot_general(
            at_row[...].astype(BF16),
            named[...].astype(BF16),
            (((1,), (1,)), ((), ())),
            preferred_element_type=F32,
        )
    half = LISTED // 2
    rest = [starts.T[:1], counts.T[:1], jnp.zeros((TABLE - half - 2, LANES), F32)]
    return [
        jnp.concatenate([table[:half]] + rest, axis=0),
        jnp.concatenate([table[half:LISTED]] + rest, axis=0),
    ]


def local_kernel(
    design_hbm, signs_hbm, sampled_hbm, owner_hbm, out_hbm,
    design, signs, sampled, owners, at_row, named, mixed, out, sems, small_sems, out_sems,
):
    chunk = ROWS // PARTS
    small = [
        pltpu.make_async_copy(source, target, small_sems.at[n])
        for n, (source, target) in enumerate(
            ((sampled_hbm, sampled), (owner_hbm, owners), (signs_hbm, signs))
        )
    ]
    copies = [
        pltpu.make_async_copy(
            design_hbm.at[pl.ds(n * chunk, chunk)], design.at[pl.ds(n * chunk, chunk)], sems.at[n]
        )
        for n in range(PARTS)
    ]
    for copy in small + copies:
        copy.start()
    order = 2 * LANES
    pairs = BLOCKS // 2
    matrix16 = sylvester(order, order).astype(BF16)
    for copy in small:
        copy.wait()
    halves = slot_table(sampled[...], owners[...], at_row, named)
    for n in range(PARTS):
        copies[n].wait()
        for pair in range(n * pairs // PARTS, (n + 1) * pairs // PARTS):
            sign = (2 * signs[2 * pair : 2 * pair + 2, :] - 1).astype(F32)
            sign16 = jnp.concatenate(
                [jnp.broadcast_to(sign[t : t + 1], (16, LANES)).astype(BF16) for t in range(2)],
                axis=1,
            )[:1]
            rows = pl.ds(pair * order, order)
            result = jnp.dot(
                design[rows, :].T * sign16, matrix16, preferred_element_type=F32
            )
            for t in range(2):
                place = (t * pairs + pair) * COLS
                mixed[place : place + COLS, :] = result[:, t * LANES : (t + 1) * LANES]

    @pl.loop(0, order // 8, unroll=2)
    def _(slab):
        first = (slab // 16) * (pairs * COLS) + (slab % 16) * 8
        transform_in_place(mixed, [aligned(first + pair * COLS, 8) for pair in range(pairs)])

    columns = COLS // PARTS

    def send(step):
        rows = aligned(step * columns * DATA, columns * DATA)
        return pltpu.make_async_copy(out.at[rows], out_hbm.at[rows], out_sems.at[step])

    @pl.loop(0, PARTS)
    def _(step):
        for part in range(BLOCKS // 8):
            for first in range(0, columns, 8):
                tile = jnp.stack(
                    [
                        mixed[aligned((part * 8 + n) * COLS + step * columns + first, 8), :]
                        for n in range(8)
                    ]
                )
                tile = jnp.swapaxes(tile, 0, 1)
                for n in range(8):
                    place = (step * columns + first + n) * DATA + part * 8
                    out[aligned(place, 8), :] = tile[n]
        for n in range(columns):
            place = (step * columns + n) * DATA + BLOCKS
            out[aligned(place, TABLE), :] = halves[n % 2]
        send(step).start()

    @pl.loop(0, PARTS)
    def _(step):
        send(step).wait()


def gather_rows(parts):
    row = iota((8, LANES), 0)
    step = 1
    while len(parts) > 1:
        upper = (row & step) != 0
        parts = [
            jnp.where(upper, b, a) + pltpu.roll(jnp.where(upper, a, b), step, 0)
            for a, b in zip(parts[0::2], parts[1::2])
        ]
        step *= 2
    return parts[0]


def mix_kernel(column_ref, out_ref):
    @pl.loop(0, BLOCKS, unroll=4)
    def _(step):
        part, low = step // 8, step % 8
        places = [high * 8 + low for high in range(16)]
        values = butterflies(
            [column_ref[aligned(place * DATA + part * 8, 8), :] for place in places]
        )
        for place, value in zip(places, values):
            out_ref[aligned(place * BLOCKS + part * 8, 8), :] = value

    @pl.loop(0, 2 * BLOCKS, unroll=4)
    def _(step):
        part, high = step // 16, step % 16
        transform_in_place(
            out_ref,
            [aligned((high * 8 + low) * BLOCKS + part * 8, 8) for low in range(8)],
        )


def pick_kernel(mixed, own_ref, other_ref, out_ref, found, picked):
    first = lax.axis_index("c") == 0
    place = iota((LANES, LANES), 0).astype(F32).astype(BF16)
    row8 = iota((8, LANES), 0)
    one, zero = jnp.ones((), BF16), jnp.zeros((), BF16)

    def samples(source):
        rows = aligned(source * TABLE, TABLE)
        own, other = own_ref[rows, :], other_ref[rows, :]
        lower, upper = jnp.where(first, own, other), jnp.where(first, other, own)
        half = LISTED // 2
        return jnp.concatenate([lower[:half], upper[:half]], axis=0).astype(jnp.int32)

    def pick_by_lanes(source):
        listed = samples(source)
        lane, block = listed & (LANES - 1), listed >> 7

        def choose(low, level):
            if level == 0:
                row = mixed[pl.ds(source * BLOCKS + low, 1), :]
                return jnp.take_along_axis(jnp.broadcast_to(row, (8, LANES)), lane, axis=1)
            a, b = choose(low, level - 1), choose(low + (1 << (level - 1)), level - 1)
            return jnp.where((block >> (level - 1)) & 1 == 1, b, a)

        found[aligned(source * LISTED, LISTED), :] = choose(0, 6)

    def pick_by_matmul(source):
        listed = samples(source)
        key = (listed & (LANES - 1)).astype(F32)
        block = listed >> 7
        values = mixed[aligned(source * BLOCKS, BLOCKS), :]
        top = values.astype(BF16)
        operand = jnp.concatenate([top, (values - top.astype(F32)).astype(BF16)], axis=0)
        parts = []
        for r in range(LISTED):
            mine = jnp.broadcast_to(key[r : r + 1], (16, LANES)).astype(BF16)
            one_hot = jnp.concatenate(
                [jnp.where(place[16 * g : 16 * g + 16] == mine, one, zero) for g in range(8)],
                axis=0,
            )
            result = jnp.dot(operand, one_hot, preferred_element_type=F32)
            wanted = jnp.broadcast_to(block[r : r + 1], (8, LANES))
            values = [
                result[8 * g : 8 * g + 8] + result[BLOCKS + 8 * g : BLOCKS + 8 * g + 8]
                for g in range(8)
            ]
            for n in range(3, 6):
                odd = (wanted >> n) & 1 == 1
                values = [jnp.where(odd, b, a) for a, b in zip(values[0::2], values[1::2])]
            parts.append(jnp.where(wanted & 7 == row8, values[0], 0.0))
        found[aligned(source * LISTED, LISTED), :] = gather_rows(parts)

    def pick(group, n):
        every = GROUP // BY_LANES if BY_LANES else GROUP + 1
        (pick_by_lanes if (n + 1) % every == 0 else pick_by_matmul)(group * GROUP + n)

    def place_in_slots(source):
        spans = own_ref[aligned(source * TABLE, TABLE), :].astype(jnp.int32)
        start, count = (jnp.broadcast_to(spans[n : n + 1], (8, LANES)) for n in (4, 5))
        here = found[aligned(source * LISTED, LISTED), :]
        for t in range(2):
            position = row8 + 8 * t
            slot = start + position
            lane = slot & (LANES - 1)
            rows = [
                jnp.take_along_axis(jnp.broadcast_to(here[r : r + 1], (8, LANES)), lane, axis=1)
                for r in range(LISTED)
            ]
            for n in range(3):
                odd = (slot >> (7 + n)) & 1 == 1
                rows = [jnp.where(odd, b, a) for a, b in zip(rows[0::2], rows[1::2])]
            picked[aligned(place_of(source) * CAP + 8 * t, 8), :] = jnp.where(
                position < count, rows[0] * SCALE, 0.0
            )

    for n in range(GROUP):
        pick(0, n)

    @pl.loop(1, DEVICES // GROUP)
    def _(group):
        for n in range(GROUP):
            place_in_slots((group - 1) * GROUP + n)
            pick(group, n)

    for n in range(GROUP):
        place_in_slots(DEVICES - GROUP + n)

    for group in range(CAP):
        out_ref[pl.ds(group, DEVICES, stride=CAP), :] = picked[
            group * LANES : (group + 1) * LANES, :
        ].T


def turn_kernel(arrived_ref, out_hbm, out, sems):
    copies = []
    for group in range(CAP):
        rows = pl.ds(group * LANES, LANES)
        out[rows, :] = arrived_ref[pl.ds(group, COLS, stride=CAP), :].T
        if group % 4 == 3:
            rows = pl.ds((group - 3) * LANES, 4 * LANES)
            copies.append(
                pltpu.make_async_copy(out.at[rows], out_hbm.at[rows], sems.at[group // 4])
            )
            copies[-1].start()
    for copy in copies:
        copy.wait()


HBM = pl.BlockSpec(memory_space=pltpu.HBM)
VMEM = pl.BlockSpec(memory_space=pltpu.VMEM)


def call(kernel, rows, specs, *args, scratch=(), limit=24, out=VMEM):
    shapes = [jax.ShapeDtypeStruct((n, LANES), F32) for n in rows]
    return pl.pallas_call(
        kernel,
        out_shape=shapes,
        in_specs=specs,
        out_specs=[out] * len(rows),
        scratch_shapes=scratch,
        compiler_params=pltpu.CompilerParams(vmem_limit_bytes=limit * 1024 * 1024),
    )(*args)


def local_call(design, sign_bits, sampled, owner_map):
    vmem, dma = pltpu.VMEM, pltpu.SemaphoreType.DMA
    return call(
        local_kernel,
        [COLS * DATA],
        [HBM] * 4,
        design,
        sign_bits.reshape(BLOCKS, LANES),
        sampled.reshape(1, SAMPLED),
        owner_map.reshape(1, SAMPLED),
        scratch=[
            vmem((ROWS, LANES), BF16),
            vmem((BLOCKS, LANES), jnp.int32),
            vmem((1, SAMPLED), jnp.int32),
            vmem((1, SAMPLED), jnp.int32),
            vmem((DEVICES, SAMPLED), F32),
            vmem((DEVICES, SAMPLED), F32),
            vmem((ROWS, LANES), F32),
            vmem((COLS * DATA, LANES), F32),
            dma((PARTS,)),
            dma((3,)),
            dma((PARTS,)),
        ],
        limit=60,
        out=HBM,
    )[0]


def mix_call(columns):
    return call(mix_kernel, [DEVICES * BLOCKS], [VMEM], columns)[0]


def pick_call(mixed, own, other):
    return call(
        pick_kernel,
        [DEVICES * CAP],
        [VMEM, VMEM, VMEM],
        mixed,
        own,
        other,
        scratch=[
            pltpu.VMEM((DEVICES * LISTED, LANES), F32),
            pltpu.VMEM((DEVICES * CAP, LANES), F32),
        ],
    )[0]


def exchange(values):
    values = values.reshape(DEVICES, 1, -1)
    return lax.all_to_all(values, ORDER, split_axis=0, concat_axis=0, tiled=True).reshape(
        -1, LANES
    )


def per_device(design, sign_bits, sampled, owner_map):
    columns = exchange(local_call(design, sign_bits, sampled, owner_map))
    own = columns.reshape(DEVICES, DATA, LANES)[:, BLOCKS:].reshape(-1, LANES)
    other = lax.ppermute(own, "c", [(0, 1), (1, 0)])
    picked = exchange(pick_call(mix_call(columns), own, other))
    (tiles,) = call(
        turn_kernel,
        [DEVICES * CAP],
        [VMEM],
        picked,
        scratch=[pltpu.VMEM((DEVICES * CAP, LANES), F32), pltpu.SemaphoreType.DMA((4,))],
        out=HBM,
    )
    return tiles.reshape(1, DEVICES, CAP, COLS)


def solution(mesh):
    in_specs = (
        P(AXES, None),
        P(AXES),
        P(AXES),
        P(AXES, None),
    )
    out_specs = P(AXES, None, None, None)
    fine = jax.sharding.Mesh(mesh.devices.reshape(SIZES), AXES)
    return jax.shard_map(
        per_device, mesh=fine, in_specs=in_specs, out_specs=out_specs, check_vma=False
    )
```

```python
import math

import jax
import jax.numpy as jnp
from jax import lax
from jax.experimental import pallas as pl
from jax.experimental.pallas import tpu as pltpu
from jax.sharding import PartitionSpec as P

AXES = ("y", "h", "z", "l", "c")
SIZES = (4, 2, 4, 2, 2)
ORDER = ("y", "z", "h", "l", "c")
DEVICES = 128
COLS = 128
LANES = 128
BLOCKS = 64
ROWS = BLOCKS * LANES
SAMPLED = 1024
CAP = 16
LISTED = SAMPLED // LANES
TABLE = 8
DATA = BLOCKS + TABLE
SCALE = 1.0 / math.sqrt(SAMPLED * DEVICES)
PARTS = 2
GROUP = 64
BY_LANES = 21
F32 = jnp.float32
BF16 = jnp.bfloat16


def iota(shape, axis):
    return lax.broadcasted_iota(jnp.int32, shape, axis)


def sylvester(rows, columns):
    common = iota((rows, columns), 0) & iota((rows, columns), 1)
    common = common ^ (common >> 4)
    common = common ^ (common >> 2)
    common = common ^ (common >> 1)
    return (1 - 2 * (common & 1)).astype(F32)


def butterflies(values):
    half = 1
    while half < len(values):
        for start in range(0, len(values), 2 * half):
            for i in range(start, start + half):
                a, b = values[i], values[i + half]
                values[i], values[i + half] = a + b, a - b
        half *= 2
    return values


def transform_in_place(ref, places):
    for place, value in zip(places, butterflies([ref[place, :] for place in places])):
        ref[place, :] = value


def aligned(start, size):
    return pl.ds(pl.multiple_of(start, 8), size)


def rank_of(place):
    return (place & 99) + ((place >> 2 & 3) << 3) + ((place >> 4 & 1) << 2)


def place_of(rank):
    return (rank & 99) + ((rank >> 3 & 3) << 2) + ((rank >> 2 & 1) << 4)


def slot_table(sampled, owners, at_row, named):
    one_hot = iota((DEVICES, SAMPLED), 0) == rank_of(owners)
    one_hot16 = one_hot.astype(F32).astype(BF16)
    upto = iota((SAMPLED, SAMPLED), 0) <= iota((SAMPLED, SAMPLED), 1)
    running = jnp.dot(one_hot16, upto.astype(F32).astype(BF16), preferred_element_type=F32)
    counts = jnp.broadcast_to(running[:, SAMPLED - 1 :], (DEVICES, LANES))
    below = iota((DEVICES, DEVICES), 1) < iota((DEVICES, DEVICES), 0)
    starts = jnp.dot(
        below.astype(F32).astype(BF16), counts.astype(BF16), preferred_element_type=F32
    )
    place = jnp.sum(
        jnp.where(one_hot, running + starts[:, :1], 0.0), axis=0, keepdims=True
    ).astype(jnp.int32) - 1
    at_row[...] = jnp.where(iota((DEVICES, SAMPLED), 0) == place >> 7, 1.0, 0.0)
    at_lane = iota((DEVICES, SAMPLED), 0) == place & (LANES - 1)
    table = jnp.zeros((DEVICES, LANES), F32)
    block = ((sampled >> 7 & 1) << 5) + (sampled >> 8)
    for part, weight in ((block, 128.0), (sampled & 127, 1.0)):
        named[...] = jnp.where(at_lane, part.astype(F32), 0.0)
        table = table + weight * lax.dot_general(
            at_row[...].astype(BF16),
            named[...].astype(BF16),
            (((1,), (1,)), ((), ())),
            preferred_element_type=F32,
        )
    half = LISTED // 2
    rest = [starts.T[:1], counts.T[:1], jnp.zeros((TABLE - half - 2, LANES), F32)]
    return [
        jnp.concatenate([table[:half]] + rest, axis=0),
        jnp.concatenate([table[half:LISTED]] + rest, axis=0),
    ]


def local_kernel(
    design_hbm, signs_hbm, sampled_hbm, owner_hbm, out_hbm,
    design, signs, sampled, owners, at_row, named, mixed, out, sems, small_sems, out_sems,
):
    chunk = ROWS // PARTS
    small = [
        pltpu.make_async_copy(source, target, small_sems.at[n])
        for n, (source, target) in enumerate(
            ((sampled_hbm, sampled), (owner_hbm, owners), (signs_hbm, signs))
        )
    ]
    copies = [
        pltpu.make_async_copy(
            design_hbm.at[pl.ds(n * chunk, chunk)], design.at[pl.ds(n * chunk, chunk)], sems.at[n]
        )
        for n in range(PARTS)
    ]
    for copy in small + copies:
        copy.start()
    order = 2 * LANES
    pairs = BLOCKS // 2
    matrix16 = sylvester(order, order).astype(BF16)
    for copy in small:
        copy.wait()
    halves = slot_table(sampled[...], owners[...], at_row, named)
    for n in range(PARTS):
        copies[n].wait()
        for pair in range(n * pairs // PARTS, (n + 1) * pairs // PARTS):
            sign = (2 * signs[2 * pair : 2 * pair + 2, :] - 1).astype(F32)
            sign16 = jnp.concatenate(
                [jnp.broadcast_to(sign[t : t + 1], (16, LANES)).astype(BF16) for t in range(2)],
                axis=1,
            )[:1]
            rows = pl.ds(pair * order, order)
            result = jnp.dot(
                design[rows, :].T * sign16, matrix16, preferred_element_type=F32
            )
            for t in range(2):
                place = (t * pairs + pair) * COLS
                mixed[place : place + COLS, :] = result[:, t * LANES : (t + 1) * LANES]

    @pl.loop(0, order // 8, unroll=2)
    def _(slab):
        first = (slab // 16) * (pairs * COLS) + (slab % 16) * 8
        transform_in_place(mixed, [aligned(first + pair * COLS, 8) for pair in range(pairs)])

    columns = COLS // PARTS

    def send(step):
        rows = aligned(step * columns * DATA, columns * DATA)
        return pltpu.make_async_copy(out.at[rows], out_hbm.at[rows], out_sems.at[step])

    @pl.loop(0, PARTS)
    def _(step):
        for part in range(BLOCKS // 8):
            for first in range(0, columns, 8):
                tile = jnp.stack(
                    [
                        mixed[aligned((part * 8 + n) * COLS + step * columns + first, 8), :]
                        for n in range(8)
                    ]
                )
                tile = jnp.swapaxes(tile, 0, 1)
                for n in range(8):
                    place = (step * columns + first + n) * DATA + part * 8
                    out[aligned(place, 8), :] = tile[n]
        for n in range(columns):
            place = (step * columns + n) * DATA + BLOCKS
            out[aligned(place, TABLE), :] = halves[n % 2]
        send(step).start()

    @pl.loop(0, PARTS)
    def _(step):
        send(step).wait()


def gather_rows(parts):
    row = iota((8, LANES), 0)
    step = 1
    while len(parts) > 1:
        upper = (row & step) != 0
        parts = [
            jnp.where(upper, b, a) + pltpu.roll(jnp.where(upper, a, b), step, 0)
            for a, b in zip(parts[0::2], parts[1::2])
        ]
        step *= 2
    return parts[0]


def mix_kernel(column_ref, out_ref):
    @pl.loop(0, BLOCKS, unroll=4)
    def _(step):
        part, low = step // 8, step % 8
        places = [high * 8 + low for high in range(16)]
        values = butterflies(
            [column_ref[aligned(place * DATA + part * 8, 8), :] for place in places]
        )
        for place, value in zip(places, values):
            out_ref[aligned(place * BLOCKS + part * 8, 8), :] = value

    @pl.loop(0, 2 * BLOCKS, unroll=4)
    def _(step):
        part, high = step // 16, step % 16
        transform_in_place(
            out_ref,
            [aligned((high * 8 + low) * BLOCKS + part * 8, 8) for low in range(8)],
        )


def pick_kernel(mixed, own_ref, other_ref, out_ref, found, picked):
    first = lax.axis_index("c") == 0
    place = iota((LANES, LANES), 0).astype(F32).astype(BF16)
    row8 = iota((8, LANES), 0)
    one, zero = jnp.ones((), BF16), jnp.zeros((), BF16)

    def samples(source):
        rows = aligned(source * TABLE, TABLE)
        own, other = own_ref[rows, :], other_ref[rows, :]
        lower, upper = jnp.where(first, own, other), jnp.where(first, other, own)
        half = LISTED // 2
        return jnp.concatenate([lower[:half], upper[:half]], axis=0).astype(jnp.int32)

    def pick_by_lanes(source):
        listed = samples(source)
        lane, block = listed & (LANES - 1), listed >> 7

        def choose(low, level):
            if level == 0:
                row = mixed[pl.ds(source * BLOCKS + low, 1), :]
                return jnp.take_along_axis(jnp.broadcast_to(row, (8, LANES)), lane, axis=1)
            a, b = choose(low, level - 1), choose(low + (1 << (level - 1)), level - 1)
            return jnp.where((block >> (level - 1)) & 1 == 1, b, a)

        found[aligned(source * LISTED, LISTED), :] = choose(0, 6)

    def pick_by_matmul(source):
        listed = samples(source)
        key = (listed & (LANES - 1)).astype(F32)
        block = listed >> 7
        values = mixed[aligned(source * BLOCKS, BLOCKS), :]
        top = values.astype(BF16)
        operand = jnp.concatenate([top, (values - top.astype(F32)).astype(BF16)], axis=0)
        parts = []
        for r in range(LISTED):
            mine = jnp.broadcast_to(key[r : r + 1], (16, LANES)).astype(BF16)
            one_hot = jnp.concatenate(
                [jnp.where(place[16 * g : 16 * g + 16] == mine, one, zero) for g in range(8)],
                axis=0,
            )
            result = jnp.dot(operand, one_hot, preferred_element_type=F32)
            wanted = jnp.broadcast_to(block[r : r + 1], (8, LANES))
            values = [
                result[8 * g : 8 * g + 8] + result[BLOCKS + 8 * g : BLOCKS + 8 * g + 8]
                for g in range(8)
            ]
            for n in range(3, 6):
                odd = (wanted >> n) & 1 == 1
                values = [jnp.where(odd, b, a) for a, b in zip(values[0::2], values[1::2])]
            parts.append(jnp.where(wanted & 7 == row8, values[0], 0.0))
        found[aligned(source * LISTED, LISTED), :] = gather_rows(parts)

    def pick(group, n):
        every = GROUP // BY_LANES if BY_LANES else GROUP + 1
        (pick_by_lanes if (n + 1) % every == 0 else pick_by_matmul)(group * GROUP + n)

    def place_in_slots(source):
        spans = own_ref[aligned(source * TABLE, TABLE), :].astype(jnp.int32)
        start, count = (jnp.broadcast_to(spans[n : n + 1], (8, LANES)) for n in (4, 5))
        here = found[aligned(source * LISTED, LISTED), :]
        for t in range(2):
            position = row8 + 8 * t
            slot = start + position
            lane = slot & (LANES - 1)
            rows = [
                jnp.take_along_axis(jnp.broadcast_to(here[r : r + 1], (8, LANES)), lane, axis=1)
                for r in range(LISTED)
            ]
            for n in range(3):
                odd = (slot >> (7 + n)) & 1 == 1
                rows = [jnp.where(odd, b, a) for a, b in zip(rows[0::2], rows[1::2])]
            picked[aligned(place_of(source) * CAP + 8 * t, 8), :] = jnp.where(
                position < count, rows[0] * SCALE, 0.0
            )

    for n in range(GROUP):
        pick(0, n)

    @pl.loop(1, DEVICES // GROUP)
    def _(group):
        for n in range(GROUP):
            place_in_slots((group - 1) * GROUP + n)
            pick(group, n)

    for n in range(GROUP):
        place_in_slots(DEVICES - GROUP + n)

    for group in range(CAP):
        out_ref[pl.ds(group, DEVICES, stride=CAP), :] = picked[
            group * LANES : (group + 1) * LANES, :
        ].T


def turn_kernel(arrived_ref, out_hbm, out, sems):
    copies = []
    for group in range(CAP):
        rows = pl.ds(group * LANES, LANES)
        out[rows, :] = arrived_ref[pl.ds(group, COLS, stride=CAP), :].T
        if group % 4 == 3:
            rows = pl.ds((group - 3) * LANES, 4 * LANES)
            copies.append(
                pltpu.make_async_copy(out.at[rows], out_hbm.at[rows], sems.at[group // 4])
            )
            copies[-1].start()
    for copy in copies:
        copy.wait()


HBM = pl.BlockSpec(memory_space=pltpu.HBM)
VMEM = pl.BlockSpec(memory_space=pltpu.VMEM)


def call(kernel, rows, specs, *args, scratch=(), limit=24, out=VMEM):
    shapes = [jax.ShapeDtypeStruct((n, LANES), F32) for n in rows]
    return pl.pallas_call(
        kernel,
        out_shape=shapes,
        in_specs=specs,
        out_specs=[out] * len(rows),
        scratch_shapes=scratch,
        compiler_params=pltpu.CompilerParams(vmem_limit_bytes=limit * 1024 * 1024),
    )(*args)


def local_call(design, sign_bits, sampled, owner_map):
    vmem, dma = pltpu.VMEM, pltpu.SemaphoreType.DMA
    return call(
        local_kernel,
        [COLS * DATA],
        [HBM] * 4,
        design,
        sign_bits.reshape(BLOCKS, LANES),
        sampled.reshape(1, SAMPLED),
        owner_map.reshape(1, SAMPLED),
        scratch=[
            vmem((ROWS, LANES), BF16),
            vmem((BLOCKS, LANES), jnp.int32),
            vmem((1, SAMPLED), jnp.int32),
            vmem((1, SAMPLED), jnp.int32),
            vmem((DEVICES, SAMPLED), F32),
            vmem((DEVICES, SAMPLED), F32),
            vmem((ROWS, LANES), F32),
            vmem((COLS * DATA, LANES), F32),
            dma((PARTS,)),
            dma((3,)),
            dma((PARTS,)),
        ],
        limit=60,
        out=HBM,
    )[0]


def mix_call(columns):
    return call(mix_kernel, [DEVICES * BLOCKS], [VMEM], columns)[0]


def pick_call(mixed, own, other):
    return call(
        pick_kernel,
        [DEVICES * CAP],
        [VMEM, VMEM, VMEM],
        mixed,
        own,
        other,
        scratch=[
            pltpu.VMEM((DEVICES * LISTED, LANES), F32),
            pltpu.VMEM((DEVICES * CAP, LANES), F32),
        ],
    )[0]


def exchange(values):
    values = values.reshape(DEVICES, 1, -1)
    return lax.all_to_all(values, ORDER, split_axis=0, concat_axis=0, tiled=True).reshape(
        -1, LANES
    )


def per_device(design, sign_bits, sampled, owner_map):
    columns = exchange(local_call(design, sign_bits, sampled, owner_map))
    own = columns.reshape(DEVICES, DATA, LANES)[:, BLOCKS:].reshape(-1, LANES)
    other = lax.ppermute(own, "c", [(0, 1), (1, 0)])
    picked = exchange(pick_call(mix_call(columns), own, other))
    (tiles,) = call(
        turn_kernel,
        [DEVICES * CAP],
        [VMEM],
        picked,
        scratch=[pltpu.VMEM((DEVICES * CAP, LANES), F32), pltpu.SemaphoreType.DMA((4,))],
        out=HBM,
    )
    return tiles.reshape(1, DEVICES, CAP, COLS)


def solution(mesh):
    in_specs = (
        P(AXES, None),
        P(AXES),
        P(AXES),
        P(AXES, None),
    )
    out_specs = P(AXES, None, None, None)
    fine = jax.sharding.Mesh(mesh.devices.reshape(SIZES), AXES)
    return jax.shard_map(
        per_device, mesh=fine, in_specs=in_specs, out_specs=out_specs, check_vma=False
    )
```
